256 devices in a mesh: tile: 64 (over z, x, core), tm: 4 (over y).
Axes of the slice: x: 4, y: 4, z: 8, core: 2. Of those that a mesh axis runs over, the one named last changes fastest.
Arguments:
- raw: bfloat16 [64, 512, 4, 1039], P('tm', 'tile'), may hold values from -600 to 600
- blocks: int32 [256], P('tile'), may hold values from 0 to 63, as said below
- mask: int32 [8, 256, 8], P('tm', 'tile'), may hold values 0 or 1
Outputs:
- correlations: float32 [8, 256, 8, 512], P('tm', 'tile')
The draws below stay inside these ranges and needn't reach their ends.
Inputs may be any that keep to these rules, and one draw needn't show every extreme that they name: `blocks`: block r belongs to tile r // 4; its partner is another tile at most 2 tiles away.
All inputs are finite; a program needn't handle non-finite values. No bound on the sum of `mask` on one device may be relied on, other than what follows from the above.
Results may differ from the reference program's by a relative error of at most 0.0077.
Values may be sent and summed in bfloat16 or wider, within the bound.
No kernel may reach another device: no remote copies, remote signals or barrier semaphores. Data moves between devices by JAX's collectives and lax.ppermute only.
A program may use at most 64 MiB of HBM per device.

```python
import math
import jax
import jax.numpy as jnp
from jax import lax

S = 8
BPD = 4
F = 512
LAGS = 512
TAPS = 64
DEC = 4
REACH = 2
TILES = 64
NSENS = 512
NBLK = 256
NWIN = 64
RAWLEN = 1039


def draw_raw(key, part):
    key = jax.random.fold_in(key, 5)
    key_base, key_sensor, key_window = jax.random.split(key, 3)
    shape = (NWIN, NSENS, DEC, RAWLEN)
    base = jnp.clip(jax.random.normal(key_base, shape, jnp.float32), -6.0, 6.0)
    spread = math.log(10.0)
    ramp = 3.0
    sensor_scale = jnp.exp(jax.random.uniform(key_sensor, (1, NSENS, 1, 1), jnp.float32) * spread)
    position = jnp.arange(NWIN).astype(jnp.float32) / max(NWIN - 1, 1)
    window_scale = (ramp ** position).reshape(NWIN, 1, 1, 1)
    window_scale = window_scale * jnp.exp(jax.random.uniform(key_window, (NWIN, 1, 1, 1), jnp.float32) * math.log(3.0))
    return (base * sensor_scale * window_scale).astype(jnp.bfloat16)


def draw_blocks(key, part):
    key = jax.random.fold_in(key, 11)
    choices_count = 2 * REACH
    scores = jax.random.randint(key, (TILES, choices_count), 0, 1000000).astype(jnp.int32)
    scores = scores * choices_count + jnp.arange(choices_count, dtype=jnp.int32)[None, :]
    order = jnp.argsort(scores, axis=1, stable=True).astype(jnp.int32)
    offset_list = jnp.concatenate([jnp.arange(-REACH, 0, dtype=jnp.int32), jnp.arange(1, REACH + 1, dtype=jnp.int32)])
    block_index = jnp.arange(NBLK, dtype=jnp.int32)
    owner = block_index // BPD
    slot = block_index % BPD
    picked = order[owner, slot]
    offset = offset_list[picked]
    forward = owner + offset
    partner = jnp.where((forward >= 0) & (forward < TILES), forward, owner - offset)
    return partner.astype(jnp.int32)


def place_ends(drawn, own_key, smallest, high):
    shape = drawn.shape
    place = [jax.random.randint(jax.random.fold_in(own_key, axis), (), 0, shape[axis]) for axis in range(len(shape))]
    drawn = drawn.at[tuple(place)].set(smallest)
    longest = shape.index(max(shape))
    place[longest] = (place[longest] + 1) % shape[longest]
    return drawn.at[tuple(place)].set(high)


def setup_inputs(seed: int = 0) -> dict:
    splits = jax.random.split(jax.random.key(seed), 4)
    return {
        "raw": draw_raw(jax.random.fold_in(splits[3], 71), 0),
        "blocks": draw_blocks(jax.random.fold_in(splits[3], 71), 0),
        "mask": place_ends((jax.random.randint(splits[2], (S, NBLK, S), 0, 5) < 3).astype(jnp.int32), jax.random.fold_in(splits[2], 1), 0, 1),
    }


def fir_taps():
    tap_index = jnp.arange(TAPS).astype(jnp.float32)
    centred = (tap_index - (TAPS - 1) / 2.0) / DEC
    taper = 0.5 - 0.5 * jnp.cos(2.0 * jnp.pi * (tap_index + 0.5) / TAPS)
    return (jnp.sinc(centred) * taper / DEC).astype(jnp.float32)

def decimate(samples, filter_taps):
    length = samples.shape[-1] - TAPS // DEC + 1
    total = jnp.zeros(samples.shape[:-2] + (length,), jnp.float32)
    for offset_index in range(TAPS // DEC):
        for phase in range(DEC):
            portion = samples[..., phase, offset_index:offset_index + length].astype(jnp.float32)
            total = total + filter_taps[DEC * offset_index + phase] * portion
    return total.astype(jnp.bfloat16)

def dft_table(length, bins):
    sample_index = jnp.arange(length)[:, None]
    bin_index = jnp.arange(bins)[None, :]
    angle = jnp.mod(sample_index * bin_index, length).astype(jnp.float32) * (2.0 * jnp.pi / length)
    return jnp.concatenate([jnp.cos(angle), -jnp.sin(angle)], axis=1).astype(jnp.bfloat16)

def lag_table(bins, lag_count, length):
    bin_index = jnp.arange(bins)[:, None]
    lag_index = jnp.arange(lag_count)[None, :] - lag_count // 2
    angle = jnp.mod(bin_index * lag_index, length).astype(jnp.float32) * (2.0 * jnp.pi / length)
    weights = jnp.where(bin_index == 0, 1.0, 2.0).astype(jnp.float32)
    return jnp.concatenate([weights * jnp.cos(angle), -weights * jnp.sin(angle)], axis=0)

def reference(raw, blocks, mask):
    filter_taps = fir_taps()
    transform = dft_table(2 * F, F).astype(jnp.float32)

    def window_spectra(window_raw):
        decimated = decimate(window_raw, filter_taps)
        product = jnp.dot(decimated.astype(jnp.float32), transform, precision=lax.Precision.HIGHEST, preferred_element_type=jnp.float32)
        return product.astype(jnp.bfloat16).reshape(NSENS, 2, F)
    spectra = lax.map(window_spectra, raw)
    real_part = spectra[:, :, 0].astype(jnp.float32)
    imag_part = spectra[:, :, 1].astype(jnp.float32)
    power = lax.optimization_barrier(jnp.sum(real_part * real_part + imag_part * imag_part, axis=0))
    amplitude = jnp.sqrt(power / NWIN + 1e-06)
    whitened = (spectra.astype(jnp.float32) / amplitude[None, :, None, :]).astype(jnp.bfloat16)
    grouped = whitened.reshape(NWIN, TILES, S, 2, F)
    lagtab = lag_table(F, LAGS, 2 * F)

    def one_block(block_index):
        own_tile = (block_index // BPD).astype(jnp.int32)
        partner_tile = blocks[block_index].astype(jnp.int32)
        own_spec = lax.dynamic_index_in_dim(grouped, own_tile, 1, keepdims=False).astype(jnp.float32)
        partner = lax.dynamic_index_in_dim(grouped, partner_tile, 1, keepdims=False).astype(jnp.float32)
        high = lax.Precision.HIGHEST
        real_cross = jnp.einsum('wif,wjf->ijf', own_spec[:, :, 0], partner[:, :, 0], precision=high) + jnp.einsum('wif,wjf->ijf', own_spec[:, :, 1], partner[:, :, 1], precision=high)
        imag_cross = jnp.einsum('wif,wjf->ijf', own_spec[:, :, 1], partner[:, :, 0], precision=high) - jnp.einsum('wif,wjf->ijf', own_spec[:, :, 0], partner[:, :, 1], precision=high)
        cross = jnp.stack([real_cross, imag_cross], axis=2).reshape(S * S, 2 * F)
        lagged = jnp.dot(cross, lagtab, precision=high, preferred_element_type=jnp.float32)
        return lagged.reshape(S, S, LAGS)
    lagged = lax.map(one_block, jnp.arange(NBLK).astype(jnp.int32))
    lagged = jnp.transpose(lagged, (1, 0, 2, 3))
    normaliser = 1.0 / jnp.sqrt(jnp.float32(NWIN * F))
    return lagged * normaliser * mask.astype(jnp.float32)[:, :, :, None]
```

```python
import functools
import math

import jax
import jax.numpy as jnp
import ml_dtypes
import numpy as np
from jax import lax
from jax.experimental import pallas as pl
from jax.experimental.pallas import tpu as pltpu
from jax.sharding import PartitionSpec as P

LAGS = 512
TAPS = 64
DEC = 4
REACH = 2
BINS = 512
LENGTH = 2 * BINS
SENSORS = 8
WIN = 16
ROWS = WIN * SENSORS
LANE = 128
SCALE = 2.0**32
PAIRS = 2 * SENSORS
CANDS = 4
MESSAGE = CANDS * PAIRS + 32
VMEM = pltpu.MemorySpace.VMEM
LIMIT = 48 * 1024 * 1024
bf16 = jnp.bfloat16
f32 = jnp.float32


def split_high_low(values):
    high = values.astype(ml_dtypes.bfloat16)
    low = (values - high.astype(np.float32)).astype(ml_dtypes.bfloat16)
    return high, low


def fir_table():
    index = np.arange(TAPS).astype(np.float64)
    centred = (index - (TAPS - 1) / 2.0) / DEC
    taper = 0.5 - 0.5 * np.cos(2.0 * np.pi * (index + 0.5) / TAPS)
    taps = (np.sinc(centred) * taper / DEC).astype(np.float32)
    high, low = split_high_low(taps)
    table = np.zeros((DEC, 2 * LANE, 2 * LANE), ml_dtypes.bfloat16)
    column = np.arange(LANE)
    for phase in range(DEC):
        for offset in range(TAPS // DEC):
            table[phase, column + offset, column] = high[DEC * offset + phase]
            table[phase, column + offset, LANE + column] = low[DEC * offset + phase]
    return table


def dft_table():
    sample = np.arange(LENGTH)[:, None]
    bins = np.arange(BINS)[None, :]
    angle = np.mod(sample * bins, LENGTH).astype(np.float64) * (2.0 * np.pi / LENGTH)
    table = np.concatenate([np.cos(angle), -np.sin(angle)], axis=1).astype(np.float32)
    return (table.astype(ml_dtypes.bfloat16).astype(np.float32) * np.float32(SCALE)).astype(
        ml_dtypes.bfloat16
    )


def lag_table():
    bins = np.arange(BINS)[:, None]
    lag = np.arange(LAGS)[None, :] - LAGS // 2
    angle = np.mod(bins * lag, LENGTH).astype(np.float64) * (2.0 * np.pi / LENGTH)
    weights = np.where(bins == 0, 1.0, 2.0)
    table = np.concatenate([weights * np.cos(angle), -weights * np.sin(angle)], axis=0)
    high, low = split_high_low(table.astype(np.float32))
    return np.stack([high, low])


def spectra_kernel(raw_ref, fir_ref, dft_ref, out_ref, wide_ref):
    blocks = LENGTH // LANE
    tail = raw_ref.shape[-1] - LENGTH
    wide_ref[blocks] = jnp.zeros((DEC * ROWS, LANE), f32)
    for row in range(ROWS):
        place = slice(row * DEC, (row + 1) * DEC)
        values = raw_ref[row // SENSORS, row % SENSORS].astype(f32)
        for k in range(blocks):
            wide_ref[k, place] = values[:, LANE * k : LANE * (k + 1)]
        wide_ref[blocks, place, :tail] = values[:, LENGTH:]
    total = jnp.zeros((SENSORS * ROWS, 2 * LANE), f32)
    for phase in range(DEC):
        samples = [
            wide_ref[k, pl.ds(phase, ROWS, stride=DEC), :].astype(bf16) for k in range(blocks + 1)
        ]
        stacked = jnp.concatenate(
            [jnp.concatenate(samples[k : k + 2], axis=1) for k in range(blocks)], axis=0
        )
        total = total + jnp.dot(stacked, fir_ref[phase], preferred_element_type=f32)
    summed = (total[:, :LANE] + total[:, LANE:]).astype(bf16)
    decimated = jnp.concatenate(
        [summed[ROWS * k : ROWS * (k + 1)] for k in range(blocks)], axis=1
    )
    out_ref[...] = jnp.dot(decimated, dft_ref[...], preferred_element_type=f32).astype(bf16)


def spectra_of(raw):
    return pl.pallas_call(
        spectra_kernel,
        out_shape=jax.ShapeDtypeStruct((ROWS, LENGTH), bf16),
        in_specs=[pl.BlockSpec(memory_space=VMEM)] * 3,
        out_specs=pl.BlockSpec(memory_space=VMEM),
        scratch_shapes=[pltpu.VMEM((LENGTH // LANE + 1, DEC * ROWS, LANE), f32)],
        compiler_params=pltpu.CompilerParams(vmem_limit_bytes=LIMIT),
        cost_estimate=pl.CostEstimate(flops=2 * 10**9, bytes_accessed=5 * 10**6, transcendentals=0),
        name="spectra",
    )(raw, jnp.asarray(fir_table()), jnp.asarray(dft_table()))


def cross_body(own_ref, far_ref, store):
    for tile in range(BINS // LANE):
        real = slice(LANE * tile, LANE * (tile + 1))
        imag = slice(BINS + LANE * tile, BINS + LANE * (tile + 1))

        def step(pair, totals):
            first, second, third, power = totals
            rows = pl.ds(pl.multiple_of(pair * 16, 16), 16)
            own_real = own_ref[rows, real].astype(f32)
            own_imag = own_ref[rows, imag].astype(f32)
            far_real = far_ref[rows, real].astype(f32)
            far_imag = far_ref[rows, imag].astype(f32)
            own_sum = own_real + own_imag
            far_difference = far_real - far_imag
            first, second, third = list(first), list(second), list(third)
            for half in range(2):
                part = slice(SENSORS * half, SENSORS * (half + 1))
                power = power + (far_real[part] * far_real[part] + far_imag[part] * far_imag[part])
                for i in range(SENSORS):
                    row = SENSORS * half + i
                    first[i] = first[i] + own_real[row : row + 1] * far_real[part]
                    second[i] = second[i] + own_imag[row : row + 1] * far_imag[part]
                    third[i] = third[i] + own_sum[row : row + 1] * far_difference[part]
            return tuple(first), tuple(second), tuple(third), power

        zero = jnp.zeros((SENSORS, LANE), f32)
        zeros = (zero,) * SENSORS
        first, second, third, power = lax.fori_loop(
            0, WIN // 2, step, (zeros, zeros, zeros, zero), unroll=True
        )
        store(real, imag, first, second, third, power)


def put_cross(out_ref, base, real, imag, first, second, third):
    for y in range(4):
        pair = [2 * y, 2 * y + 1]
        real_cross = jnp.concatenate([first[i] + second[i] for i in pair], axis=0)
        imag_cross = jnp.concatenate([third[i] - first[i] + second[i] for i in pair], axis=0)
        out_ref[y, base : base + PAIRS, real] = real_cross.astype(bf16)
        out_ref[y, base : base + PAIRS, imag] = imag_cross.astype(bf16)


def cross_kernel(own_ref, far_ref, out_ref, power_ref):
    def store(real, imag, first, second, third, power):
        put_cross(out_ref, 0, real, imag, first, second, third)
        power_ref[:, real] = power

    cross_body(own_ref, far_ref, store)


def cross_of(own, far):
    return pl.pallas_call(
        cross_kernel,
        out_shape=(
            jax.ShapeDtypeStruct((4, PAIRS, LENGTH), bf16),
            jax.ShapeDtypeStruct((SENSORS, BINS), f32),
        ),
        in_specs=[pl.BlockSpec(memory_space=VMEM)] * 2,
        out_specs=(pl.BlockSpec(memory_space=VMEM),) * 2,
        compiler_params=pltpu.CompilerParams(vmem_limit_bytes=LIMIT),
        cost_estimate=pl.CostEstimate(flops=10**8, bytes_accessed=10**6, transcendentals=0),
        name="cross",
    )(own, far)


def message_kernel(own_ref, third_ref, fourth_ref, s_ref, sp_ref, a_ref, ap_ref, out_ref):
    for y in range(4):
        out_ref[y, 0:PAIRS] = s_ref[y]
        out_ref[y, PAIRS : 2 * PAIRS] = a_ref[y]
    base = CANDS * PAIRS
    own_power = jnp.zeros((SENSORS, BINS), f32)
    for w in range(WIN // 2):
        block = own_ref[16 * w : 16 * (w + 1)].astype(f32)
        square = block * block
        square = square[:SENSORS] + square[SENSORS:]
        own_power = own_power + (square[:, :BINS] + square[:, BINS:])
    powers = {0: sp_ref[...], 1: ap_ref[...]}
    for slot, far_ref in ((2, third_ref), (3, fourth_ref)):
        collected = []

        def store(real, imag, first, second, third, power):
            put_cross(out_ref, slot * PAIRS, real, imag, first, second, third)
            collected.append(power)

        cross_body(own_ref, far_ref, store)
        powers[slot] = jnp.concatenate(collected, axis=1)
    near = jnp.concatenate(
        [
            jnp.concatenate([powers[0], powers[1]], axis=1),
            jnp.concatenate([powers[2], powers[3]], axis=1),
        ],
        axis=0,
    ).astype(bf16)
    high = own_power.astype(bf16)
    low = (own_power - high.astype(f32)).astype(bf16)
    mine = jnp.concatenate([high, low], axis=1)
    mine = jnp.concatenate([mine, mine], axis=0)
    for y in range(4):
        out_ref[y, base : base + 16] = near
        out_ref[y, base + 16 : base + 32] = mine


def message_of(own, third, fourth, s_cross, s_power, a_cross, a_power):
    return pl.pallas_call(
        message_kernel,
        out_shape=jax.ShapeDtypeStruct((4, MESSAGE, LENGTH), bf16),
        in_specs=[pl.BlockSpec(memory_space=VMEM)] * 7,
        out_specs=pl.BlockSpec(memory_space=VMEM),
        compiler_params=pltpu.CompilerParams(vmem_limit_bytes=LIMIT),
        cost_estimate=pl.CostEstimate(flops=2 * 10**8, bytes_accessed=10**6, transcendentals=0),
        name="message",
    )(own, third, fourth, s_cross, s_power, a_cross, a_power)


def lag_kernel(slots_ref, position_ref, got_ref, table_ref, mask_ref, out_ref, lagged_ref):
    base = CANDS * PAIRS

    def summed(rows):
        return (got_ref[0, rows].astype(f32) + got_ref[1, rows].astype(f32)) + (
            got_ref[2, rows].astype(f32) + got_ref[3, rows].astype(f32)
        )

    def inverse(power):
        return lax.rsqrt(power / (4 * WIN) + 1e-06 * SCALE * SCALE)

    near = inverse(summed(slice(base, base + 16)))
    mine = summed(slice(base + 16, base + 32))[:SENSORS]
    mine = inverse(mine[:, :BINS] + mine[:, BINS:])
    y = position_ref[0]
    sensor = lax.broadcasted_iota(jnp.int32, (SENSORS, BINS), 0)
    own = [
        jnp.sum(jnp.where(sensor == 2 * y + i, mine, 0.0), axis=0, keepdims=True) for i in range(2)
    ]
    pieces = []
    for slot in range(CANDS):
        row, column = slot // 2, slot % 2
        far = near[SENSORS * row : SENSORS * (row + 1), BINS * column : BINS * (column + 1)]
        cross = summed(slice(slot * PAIRS, (slot + 1) * PAIRS))
        for i in range(2):
            factor = far * own[i]
            factor = jnp.concatenate([factor, factor], axis=1)
            pieces.append(cross[SENSORS * i : SENSORS * (i + 1)] * factor)
    whitened = jnp.concatenate(pieces, axis=0)
    high = whitened.astype(bf16)
    low = (whitened - high.astype(f32)).astype(bf16)
    lagged = jnp.dot(high, table_ref[0], preferred_element_type=f32)
    lagged = lagged + jnp.dot(high, table_ref[1], preferred_element_type=f32)
    lagged = lagged + jnp.dot(low, table_ref[0], preferred_element_type=f32)
    lagged_ref[...] = lagged.reshape(CANDS, 2, SENSORS, LAGS)
    normaliser = 1.0 / math.sqrt(4 * WIN * BINS)
    for r in range(4):
        slot = slots_ref[r]
        for i in range(2):
            factor = mask_ref[i, r] * normaliser
            for k in range(LAGS // LANE):
                lanes = slice(LANE * k, LANE * (k + 1))
                out_ref[i, r, :, lanes] = lagged_ref[slot, i, :, lanes] * factor


def lag_of(slots, position, got, mask):
    smem = pl.BlockSpec(memory_space=pltpu.MemorySpace.SMEM)
    vmem = pl.BlockSpec(memory_space=VMEM)
    return pl.pallas_call(
        lag_kernel,
        out_shape=jax.ShapeDtypeStruct((2, 4, SENSORS, LAGS), f32),
        in_specs=[smem, smem, vmem, vmem, vmem],
        out_specs=vmem,
        scratch_shapes=[pltpu.VMEM((CANDS, 2, SENSORS, LAGS), f32)],
        compiler_params=pltpu.CompilerParams(vmem_limit_bytes=LIMIT),
        cost_estimate=pl.CostEstimate(flops=2 * 10**8, bytes_accessed=3 * 10**6, transcendentals=0),
        name="lag",
    )(slots, position, got, jnp.asarray(lag_table()), mask)


def per_device(raw, blocks, mask):
    tiles = lax.axis_size("tile")
    tile = lax.axis_index("tile")
    core = tile % 2
    relative = blocks - tile
    other = 1 - 2 * core
    slots = jnp.where(
        relative == other,
        0,
        jnp.where(relative == -other, 3, jnp.where(relative == 2 * other, 1, 2)),
    ).astype(jnp.int32)
    position = lax.axis_index("tm").astype(jnp.int32).reshape(1)
    wide_mask = jnp.broadcast_to(mask.astype(f32)[..., None], mask.shape + (LANE,))

    def ring(block, distances):
        route = [(i, (i + distances[i % 2]) % tiles) for i in range(tiles)]
        return lax.ppermute(block, "tile", route)

    spectra = spectra_of(raw)
    near = ring(spectra, (1, -1))
    ahead = ring(spectra, (-2, 2))
    behind = ring(spectra, (2, -2))
    corner = ring(ahead, (1, -1))
    s_cross, s_power = cross_of(spectra, near)
    a_cross, a_power = cross_of(spectra, ahead)
    message = message_of(spectra, behind, corner, s_cross, s_power, a_cross, a_power)
    got = lax.all_to_all(message, "tm", 0, 0)
    return lag_of(slots, position, got, wide_mask)


def solution(mesh):
    placed = (P("tm", "tile", None, None), P("tile"), P("tm", "tile", None))
    return jax.shard_map(
        per_device,
        mesh=mesh,
        in_specs=placed,
        out_specs=P("tm", "tile", None, None),
        check_vma=False,
    )
```

```python
import functools
import math

import jax
import jax.numpy as jnp
import ml_dtypes
import numpy as np
from jax import lax
from jax.experimental import pallas as pl
from jax.experimental.pallas import tpu as pltpu
from jax.sharding import PartitionSpec as P

LAGS = 512
TAPS = 64
DEC = 4
REACH = 2
BINS = 512
LENGTH = 2 * BINS
SENSORS = 8
WIN = 16
ROWS = WIN * SENSORS
LANE = 128
SCALE = 2.0**32
PAIRS = 2 * SENSORS
CANDS = 4
MESSAGE = CANDS * PAIRS + 32
VMEM = pltpu.MemorySpace.VMEM
CHUNKS = 4
LIMIT = 48 * 1024 * 1024
WHOLE = 62 * 1024 * 1024
bf16 = jnp.bfloat16
f32 = jnp.float32


def split_high_low(values):
    high = values.astype(ml_dtypes.bfloat16)
    low = (values - high.astype(np.float32)).astype(ml_dtypes.bfloat16)
    return high, low


def fir_table():
    index = np.arange(TAPS).astype(np.float64)
    centred = (index - (TAPS - 1) / 2.0) / DEC
    taper = 0.5 - 0.5 * np.cos(2.0 * np.pi * (index + 0.5) / TAPS)
    taps = (np.sinc(centred) * taper / DEC).astype(np.float32)
    high, low = split_high_low(taps)
    table = np.zeros((DEC, 2 * LANE, 2 * LANE), ml_dtypes.bfloat16)
    column = np.arange(LANE)
    for phase in range(DEC):
        for offset in range(TAPS // DEC):
            table[phase, column + offset, column] = high[DEC * offset + phase]
            table[phase, column + offset, LANE + column] = low[DEC * offset + phase]
    return table


def dft_table():
    sample = np.arange(LENGTH)[:, None]
    bins = np.arange(BINS)[None, :]
    angle = np.mod(sample * bins, LENGTH).astype(np.float64) * (2.0 * np.pi / LENGTH)
    table = np.concatenate([np.cos(angle), -np.sin(angle)], axis=1).astype(np.float32)
    return (table.astype(ml_dtypes.bfloat16).astype(np.float32) * np.float32(SCALE)).astype(
        ml_dtypes.bfloat16
    )


def lag_table():
    bins = np.arange(BINS)[:, None]
    lag = np.arange(LAGS)[None, :] - LAGS // 2
    angle = np.mod(bins * lag, LENGTH).astype(np.float64) * (2.0 * np.pi / LENGTH)
    weights = np.where(bins == 0, 1.0, 2.0)
    table = np.concatenate([weights * np.cos(angle), -weights * np.sin(angle)], axis=0)
    high, low = split_high_low(table.astype(np.float32))
    return np.stack([high, low])


def spectra_kernel(
    raw_hbm, fir_hbm, dft_hbm, out_ref, raw_ref, fir_ref, dft_ref, wide_ref, sems
):
    def fetch(source, target, index):
        return pltpu.make_async_copy(source, target, sems.at[index])

    windows = raw_ref.shape[0] // CHUNKS
    depth = LENGTH // CHUNKS
    raw_copies = [
        fetch(
            raw_hbm.at[pl.ds(windows * c, windows)], raw_ref.at[pl.ds(windows * c, windows)], c
        )
        for c in range(CHUNKS)
    ]
    fir_copy = fetch(fir_hbm, fir_ref, CHUNKS)
    dft_copies = [
        fetch(
            dft_hbm.at[pl.ds(depth * c, depth)],
            dft_ref.at[pl.ds(depth * c, depth)],
            CHUNKS + 1 + c,
        )
        for c in range(CHUNKS)
    ]
    for copy in raw_copies + [fir_copy] + dft_copies:
        copy.start()
    blocks = LENGTH // LANE
    tail = raw_ref.shape[-1] - LENGTH
    wide_ref[blocks] = jnp.zeros((DEC * ROWS, LANE), f32)
    for c in range(CHUNKS):
        raw_copies[c].wait()
        for row in range(windows * SENSORS * c, windows * SENSORS * (c + 1)):
            place = slice(row * DEC, (row + 1) * DEC)
            values = raw_ref[row // SENSORS, row % SENSORS].astype(f32)
            for k in range(blocks):
                wide_ref[k, place] = values[:, LANE * k : LANE * (k + 1)]
            wide_ref[blocks, place, :tail] = values[:, LENGTH:]
    fir_copy.wait()
    total = jnp.zeros((SENSORS * ROWS, 2 * LANE), f32)
    for phase in range(DEC):
        samples = [
            wide_ref[k, pl.ds(phase, ROWS, stride=DEC), :].astype(bf16) for k in range(blocks + 1)
        ]
        stacked = jnp.concatenate(
            [jnp.concatenate(samples[k : k + 2], axis=1) for k in range(blocks)], axis=0
        )
        total = total + jnp.dot(stacked, fir_ref[phase], preferred_element_type=f32)
    summed = (total[:, :LANE] + total[:, LANE:]).astype(bf16)
    decimated = jnp.concatenate(
        [summed[ROWS * k : ROWS * (k + 1)] for k in range(blocks)], axis=1
    )
    for copy in dft_copies:
        copy.wait()
    spectra = jnp.dot(decimated, dft_ref[...], preferred_element_type=f32)
    out_ref[...] = spectra.astype(bf16)


def spectra_of(raw):
    hbm = pl.BlockSpec(memory_space=pltpu.MemorySpace.HBM)
    fir, dft = fir_table(), dft_table()
    return pl.pallas_call(
        spectra_kernel,
        out_shape=jax.ShapeDtypeStruct((ROWS, LENGTH), bf16),
        in_specs=[hbm, hbm, hbm],
        out_specs=pl.BlockSpec(memory_space=VMEM),
        scratch_shapes=[
            pltpu.VMEM(raw.shape, bf16),
            pltpu.VMEM(fir.shape, bf16),
            pltpu.VMEM(dft.shape, bf16),
            pltpu.VMEM((LENGTH // LANE + 1, DEC * ROWS, LANE), f32),
            pltpu.SemaphoreType.DMA((2 * CHUNKS + 1,)),
        ],
        compiler_params=pltpu.CompilerParams(vmem_limit_bytes=WHOLE),
        cost_estimate=pl.CostEstimate(flops=2 * 10**9, bytes_accessed=5 * 10**6, transcendentals=0),
        name="spectra",
    )(raw, jnp.asarray(fir), jnp.asarray(dft))


def cross_body(own_ref, far_ref, store):
    for tile in range(BINS // LANE):
        real = slice(LANE * tile, LANE * (tile + 1))
        imag = slice(BINS + LANE * tile, BINS + LANE * (tile + 1))

        def step(pair, totals):
            first, second, third, power = totals
            rows = pl.ds(pl.multiple_of(pair * 16, 16), 16)
            own_real = own_ref[rows, real]
            own_imag = own_ref[rows, imag]
            far_real = far_ref[rows, real].astype(f32)
            far_imag = far_ref[rows, imag].astype(f32)
            own_sum = own_real + own_imag
            far_difference = far_real - far_imag
            first, second, third = list(first), list(second), list(third)
            for half in range(2):
                part = slice(SENSORS * half, SENSORS * (half + 1))
                power = power + (far_real[part] * far_real[part] + far_imag[part] * far_imag[part])
                for i in range(SENSORS):
                    row = SENSORS * half + i
                    first[i] = first[i] + own_real[row : row + 1] * far_real[part]
                    second[i] = second[i] + own_imag[row : row + 1] * far_imag[part]
                    third[i] = third[i] + own_sum[row : row + 1] * far_difference[part]
            return tuple(first), tuple(second), tuple(third), power

        zero = jnp.zeros((SENSORS, LANE), f32)
        zeros = (zero,) * SENSORS
        first, second, third, power = lax.fori_loop(
            0, WIN // 2, step, (zeros, zeros, zeros, zero), unroll=True
        )
        store(real, imag, first, second, third, power)


def put_cross(out_refs, base, real, imag, first, second, third):
    for k in range(4):
        pair = [2 * k, 2 * k + 1]
        real_cross = jnp.concatenate([first[i] + second[i] for i in pair], axis=0)
        imag_cross = jnp.concatenate([third[i] - first[i] + second[i] for i in pair], axis=0)
        out_refs[k][base : base + PAIRS, real] = real_cross.astype(bf16)
        out_refs[k][base : base + PAIRS, imag] = imag_cross.astype(bf16)


def cross_kernel(own_ref, far_ref, out_ref, power_ref):
    def store(real, imag, first, second, third, power):
        put_cross([out_ref.at[k] for k in range(4)], 0, real, imag, first, second, third)
        power_ref[:, real] = power

    cross_body(own_ref, far_ref, store)


def cross_of(own, far):
    return pl.pallas_call(
        cross_kernel,
        out_shape=(
            jax.ShapeDtypeStruct((4, PAIRS, LENGTH), bf16),
            jax.ShapeDtypeStruct((SENSORS, BINS), f32),
        ),
        in_specs=[pl.BlockSpec(memory_space=VMEM)] * 2,
        out_specs=(pl.BlockSpec(memory_space=VMEM),) * 2,
        compiler_params=pltpu.CompilerParams(vmem_limit_bytes=LIMIT),
        cost_estimate=pl.CostEstimate(flops=10**8, bytes_accessed=10**6, transcendentals=0),
        name="cross",
    )(own, far)


def own_kernel(turn_ref, spectra_ref, own_ref, mine_ref):
    shift = lax.rem(SENSORS - 2 * turn_ref[0], SENSORS)
    power = jnp.zeros((SENSORS, BINS), f32)
    for window in range(WIN):
        rows = slice(SENSORS * window, SENSORS * (window + 1))
        block = pltpu.roll(spectra_ref[rows].astype(f32), shift, 0)
        own_ref[rows] = block
        square = block * block
        power = power + (square[:, :BINS] + square[:, BINS:])
    high = power.astype(bf16).astype(f32)
    mine = jnp.concatenate([high, power - high], axis=1)
    for k in range(4):
        mine_ref[k] = jnp.concatenate([mine[2 * k : 2 * k + 2]] * SENSORS, axis=0).astype(bf16)


def own_of(turn, spectra):
    vmem = pl.BlockSpec(memory_space=VMEM)
    return pl.pallas_call(
        own_kernel,
        out_shape=(
            jax.ShapeDtypeStruct((ROWS, LENGTH), f32),
            jax.ShapeDtypeStruct((4, 16, LENGTH), bf16),
        ),
        in_specs=[pl.BlockSpec(memory_space=pltpu.MemorySpace.SMEM), vmem],
        out_specs=(vmem, vmem),
        compiler_params=pltpu.CompilerParams(vmem_limit_bytes=LIMIT),
        cost_estimate=pl.CostEstimate(flops=10**6, bytes_accessed=10**6, transcendentals=0),
        name="own",
    )(turn, spectra)


def message_kernel(
    own_ref, third_ref, fourth_ref, s_ref, sp_ref, a_ref, ap_ref, mine_ref, *out_refs
):
    powers = {0: sp_ref[...], 1: ap_ref[...]}
    for slot, far_ref in ((2, third_ref), (3, fourth_ref)):
        collected = []

        def store(real, imag, first, second, third, power):
            put_cross(out_refs, slot * PAIRS, real, imag, first, second, third)
            collected.append(power)

        cross_body(own_ref, far_ref, store)
        powers[slot] = jnp.concatenate(collected, axis=1)
    near = jnp.concatenate(
        [
            jnp.concatenate([powers[0], powers[1]], axis=1),
            jnp.concatenate([powers[2], powers[3]], axis=1),
        ],
        axis=0,
    ).astype(bf16)
    base = CANDS * PAIRS
    for k in range(4):
        out_refs[k][0:PAIRS] = s_ref[k]
        out_refs[k][PAIRS : 2 * PAIRS] = a_ref[k]
        out_refs[k][base : base + 16] = near
        out_refs[k][base + 16 : base + 32] = mine_ref[k]


def messages_of(*parts):
    vmem = pl.BlockSpec(memory_space=VMEM)
    return pl.pallas_call(
        message_kernel,
        out_shape=(jax.ShapeDtypeStruct((MESSAGE, LENGTH), bf16),) * 4,
        in_specs=[vmem] * 8,
        out_specs=(vmem,) * 4,
        compiler_params=pltpu.CompilerParams(vmem_limit_bytes=LIMIT),
        cost_estimate=pl.CostEstimate(flops=2 * 10**8, bytes_accessed=10**6, transcendentals=0),
        name="message",
    )(*parts)


def lag_kernel(slots_ref, table_ref, mask_ref, *refs):
    got_refs, out_ref, lagged_ref = refs[:4], refs[4], refs[5]
    base = CANDS * PAIRS

    def summed(rows):
        parts = [ref[rows].astype(f32) for ref in got_refs]
        return (parts[0] + parts[1]) + (parts[2] + parts[3])

    def inverse(power):
        return lax.rsqrt(power / (4 * WIN) + 1e-06 * SCALE * SCALE)

    near = inverse(summed(slice(base, base + 16)))
    mine = summed(slice(base + 16, base + 32))
    mine = inverse(mine[:, :BINS] + mine[:, BINS:])
    own = [mine[i : i + 1] for i in range(2)]
    pieces = []
    for slot in range(CANDS):
        row, column = slot // 2, slot % 2
        far = near[SENSORS * row : SENSORS * (row + 1), BINS * column : BINS * (column + 1)]
        cross = summed(slice(slot * PAIRS, (slot + 1) * PAIRS))
        for i in range(2):
            factor = far * own[i]
            factor = jnp.concatenate([factor, factor], axis=1)
            pieces.append(cross[SENSORS * i : SENSORS * (i + 1)] * factor)
    whitened = jnp.concatenate(pieces, axis=0)
    high = whitened.astype(bf16)
    low = (whitened - high.astype(f32)).astype(bf16)
    both = jnp.concatenate([high, low], axis=0)
    lagged = jnp.dot(both, table_ref[0], preferred_element_type=f32)
    lagged = lagged[: CANDS * PAIRS] + lagged[CANDS * PAIRS :]
    lagged = lagged + jnp.dot(high, table_ref[1], preferred_element_type=f32)
    lagged_ref[...] = lagged.reshape(CANDS, 2, SENSORS, LAGS)
    normaliser = 1.0 / math.sqrt(4 * WIN * BINS)
    for r in range(4):
        slot = slots_ref[r]
        for i in range(2):
            factor = mask_ref[i, r] * normaliser
            for k in range(LAGS // LANE):
                lanes = slice(LANE * k, LANE * (k + 1))
                out_ref[i, r, :, lanes] = lagged_ref[slot, i, :, lanes] * factor


def lag_of(slots, mask, *got):
    smem = pl.BlockSpec(memory_space=pltpu.MemorySpace.SMEM)
    vmem = pl.BlockSpec(memory_space=VMEM)
    return pl.pallas_call(
        lag_kernel,
        out_shape=jax.ShapeDtypeStruct((2, 4, SENSORS, LAGS), f32),
        in_specs=[smem] + [vmem] * 6,
        out_specs=vmem,
        scratch_shapes=[pltpu.VMEM((CANDS, 2, SENSORS, LAGS), f32)],
        compiler_params=pltpu.CompilerParams(vmem_limit_bytes=LIMIT),
        cost_estimate=pl.CostEstimate(flops=2 * 10**8, bytes_accessed=3 * 10**6, transcendentals=0),
        name="lag",
    )(slots, jnp.asarray(lag_table()), mask, *got)


def per_device(raw, blocks, mask):
    tiles = lax.axis_size("tile")
    tile = lax.axis_index("tile")
    core = tile % 2
    relative = blocks - tile
    other = 1 - 2 * core
    slots = jnp.where(
        relative == other,
        0,
        jnp.where(relative == -other, 3, jnp.where(relative == 2 * other, 1, 2)),
    ).astype(jnp.int32)
    turn = lax.axis_index("tm").astype(jnp.int32).reshape(1)
    wide_mask = jnp.broadcast_to(mask.astype(f32)[..., None], mask.shape + (LANE,))

    def ring(block, distances):
        route = [(i, (i + distances[i % 2]) % tiles) for i in range(tiles)]
        return lax.ppermute(block, "tile", route)

    def onward(block, distance):
        groups = lax.axis_size("tm")
        return lax.ppermute(block, "tm", [(i, (i + distance) % groups) for i in range(groups)])

    spectra = spectra_of(raw)
    near = ring(spectra, (1, -1))
    ahead = ring(spectra, (-2, 2))
    behind = ring(spectra, (2, -2))
    corner = ring(ahead, (1, -1))
    own, mine = own_of(turn, spectra)
    s_cross, s_power = cross_of(own, near)
    a_cross, a_power = cross_of(own, ahead)
    messages = messages_of(
        own, behind, corner, s_cross, s_power, a_cross, a_power, mine
    )
    got = [messages[0]] + [onward(messages[k], k) for k in (2, 1, 3)]
    return lag_of(slots, wide_mask, *got)


def solution(mesh):
    placed = (P("tm", "tile", None, None), P("tile"), P("tm", "tile", None))
    return jax.shard_map(
        per_device,
        mesh=mesh,
        in_specs=placed,
        out_specs=P("tm", "tile", None, None),
        check_vma=False,
    )
```

```python
import functools
import math

import jax
import jax.numpy as jnp
import ml_dtypes
import numpy as np
from jax import lax
from jax.experimental import pallas as pl
from jax.experimental.pallas import tpu as pltpu
from jax.sharding import PartitionSpec as P

LAGS = 512
TAPS = 64
DEC = 4
REACH = 2
BINS = 512
LENGTH = 2 * BINS
SENSORS = 8
WIN = 16
ROWS = WIN * SENSORS
LANE = 128
SCALE = 2.0**32
PAIRS = 2 * SENSORS
CANDS = 4
MESSAGE = CANDS * PAIRS + 32
VMEM = pltpu.MemorySpace.VMEM
CHUNKS = 4
LAG_PASSES = 2
LIMIT = 16 * 1024 * 1024
bf16 = jnp.bfloat16
f32 = jnp.float32


def split_high_low(values):
    high = values.astype(ml_dtypes.bfloat16)
    low = (values - high.astype(np.float32)).astype(ml_dtypes.bfloat16)
    return high, low


def fir_table():
    index = np.arange(TAPS).astype(np.float64)
    centred = (index - (TAPS - 1) / 2.0) / DEC
    taper = 0.5 - 0.5 * np.cos(2.0 * np.pi * (index + 0.5) / TAPS)
    taps = (np.sinc(centred) * taper / DEC).astype(np.float32)
    high, low = split_high_low(taps)
    table = np.zeros((DEC, 2 * LANE, 2 * LANE), ml_dtypes.bfloat16)
    column = np.arange(LANE)
    for phase in range(DEC):
        for offset in range(TAPS // DEC):
            table[phase, column + offset, column] = high[DEC * offset + phase]
            table[phase, column + offset, LANE + column] = low[DEC * offset + phase]
    return table


def dft_table():
    sample = np.arange(LENGTH)[:, None]
    bins = np.arange(BINS)[None, :]
    angle = np.mod(sample * bins, LENGTH).astype(np.float64) * (2.0 * np.pi / LENGTH)
    table = np.concatenate([np.cos(angle), -np.sin(angle)], axis=1).astype(np.float32)
    return (table.astype(ml_dtypes.bfloat16).astype(np.float32) * np.float32(SCALE)).astype(
        ml_dtypes.bfloat16
    )


def lag_table():
    bins = np.arange(BINS)[:, None]
    lag = np.arange(LAGS)[None, :] - LAGS // 2
    angle = np.mod(bins * lag, LENGTH).astype(np.float64) * (2.0 * np.pi / LENGTH)
    weights = np.where(bins == 0, 1.0, 2.0)
    table = np.concatenate([weights * np.cos(angle), -weights * np.sin(angle)], axis=0)
    high, low = split_high_low(table.astype(np.float32))
    return np.stack([high, low])


def spectra_kernel(
    raw_hbm, fir_hbm, dft_hbm, out_ref, raw_ref, fir_ref, dft_ref, wide_ref, sems
):
    def fetch(source, target, index):
        return pltpu.make_async_copy(source, target, sems.at[index])

    windows = raw_ref.shape[0] // CHUNKS
    depth = LENGTH // CHUNKS
    raw_copies = [
        fetch(
            raw_hbm.at[pl.ds(windows * c, windows)], raw_ref.at[pl.ds(windows * c, windows)], c
        )
        for c in range(CHUNKS)
    ]
    fir_copy = fetch(fir_hbm, fir_ref, CHUNKS)
    dft_copies = [
        fetch(
            dft_hbm.at[pl.ds(depth * c, depth)],
            dft_ref.at[pl.ds(depth * c, depth)],
            CHUNKS + 1 + c,
        )
        for c in range(CHUNKS)
    ]
    for copy in raw_copies + [fir_copy] + dft_copies:
        copy.start()
    blocks = LENGTH // LANE
    tail = raw_ref.shape[-1] - LENGTH
    wide_ref[blocks] = jnp.zeros((DEC * ROWS, LANE), f32)
    for c in range(CHUNKS):
        raw_copies[c].wait()
        for row in range(windows * SENSORS * c, windows * SENSORS * (c + 1)):
            place = slice(row * DEC, (row + 1) * DEC)
            values = raw_ref[row // SENSORS, row % SENSORS].astype(f32)
            for k in range(blocks):
                wide_ref[k, place] = values[:, LANE * k : LANE * (k + 1)]
            wide_ref[blocks, place, :tail] = values[:, LENGTH:]
    fir_copy.wait()
    total = jnp.zeros((SENSORS * ROWS, 2 * LANE), f32)
    for phase in range(DEC):
        samples = [
            wide_ref[k, pl.ds(phase, ROWS, stride=DEC), :].astype(bf16) for k in range(blocks + 1)
        ]
        stacked = jnp.concatenate(
            [jnp.concatenate(samples[k : k + 2], axis=1) for k in range(blocks)], axis=0
        )
        total = total + jnp.dot(stacked, fir_ref[phase], preferred_element_type=f32)
    summed = (total[:, :LANE] + total[:, LANE:]).astype(bf16)
    decimated = jnp.concatenate(
        [summed[ROWS * k : ROWS * (k + 1)] for k in range(blocks)], axis=1
    )
    for copy in dft_copies:
        copy.wait()
    spectra = jnp.dot(decimated, dft_ref[...], preferred_element_type=f32)
    out_ref[...] = spectra.astype(bf16)


def in_hbm(array):
    return pltpu.with_memory_space_constraint(array, pltpu.MemorySpace.HBM)


def spectra_of(raw):
    hbm = pl.BlockSpec(memory_space=pltpu.MemorySpace.HBM)
    fir, dft = fir_table(), dft_table()
    return pl.pallas_call(
        spectra_kernel,
        out_shape=pltpu.VMEM((ROWS, LENGTH), bf16),
        in_specs=[hbm, hbm, hbm],
        out_specs=pl.BlockSpec(memory_space=VMEM),
        scratch_shapes=[
            pltpu.VMEM(raw.shape, bf16),
            pltpu.VMEM(fir.shape, bf16),
            pltpu.VMEM(dft.shape, bf16),
            pltpu.VMEM((LENGTH // LANE + 1, DEC * ROWS, LANE), f32),
            pltpu.SemaphoreType.DMA((2 * CHUNKS + 1,)),
        ],
        compiler_params=pltpu.CompilerParams(vmem_limit_bytes=LIMIT),
        cost_estimate=pl.CostEstimate(flops=10**5, bytes_accessed=10**4, transcendentals=0),
        name="spectra",
    )(in_hbm(raw), in_hbm(jnp.asarray(fir)), in_hbm(jnp.asarray(dft)))


def cross_body(own_ref, far_ref, store):
    for tile in range(BINS // LANE):
        real = slice(LANE * tile, LANE * (tile + 1))
        imag = slice(BINS + LANE * tile, BINS + LANE * (tile + 1))

        def step(pair, totals):
            first, second, third, power = totals
            rows = pl.ds(pl.multiple_of(pair * 16, 16), 16)
            own_real = own_ref[rows, real]
            own_imag = own_ref[rows, imag]
            far_real = far_ref[rows, real].astype(f32)
            far_imag = far_ref[rows, imag].astype(f32)
            own_sum = own_real + own_imag
            far_difference = far_real - far_imag
            first, second, third = list(first), list(second), list(third)
            for half in range(2):
                part = slice(SENSORS * half, SENSORS * (half + 1))
                power = power + (far_real[part] * far_real[part] + far_imag[part] * far_imag[part])
                for i in range(SENSORS):
                    row = SENSORS * half + i
                    first[i] = first[i] + own_real[row : row + 1] * far_real[part]
                    second[i] = second[i] + own_imag[row : row + 1] * far_imag[part]
                    third[i] = third[i] + own_sum[row : row + 1] * far_difference[part]
            return tuple(first), tuple(second), tuple(third), power

        zero = jnp.zeros((SENSORS, LANE), f32)
        zeros = (zero,) * SENSORS
        first, second, third, power = lax.fori_loop(
            0, WIN // 2, step, (zeros, zeros, zeros, zero), unroll=True
        )
        store(real, imag, first, second, third, power)


def put_cross(out_refs, base, real, imag, first, second, third):
    for k in range(4):
        pair = [2 * k, 2 * k + 1]
        real_cross = jnp.concatenate([first[i] + second[i] for i in pair], axis=0)
        imag_cross = jnp.concatenate([third[i] - first[i] + second[i] for i in pair], axis=0)
        out_refs[k][base : base + PAIRS, real] = real_cross.astype(bf16)
        out_refs[k][base : base + PAIRS, imag] = imag_cross.astype(bf16)


def cross_kernel(own_ref, far_ref, out_ref, power_ref):
    def store(real, imag, first, second, third, power):
        put_cross([out_ref.at[k] for k in range(4)], 0, real, imag, first, second, third)
        power_ref[:, real] = power

    cross_body(own_ref, far_ref, store)


def cross_of(own, far):
    return pl.pallas_call(
        cross_kernel,
        out_shape=(
            pltpu.VMEM((4, PAIRS, LENGTH), bf16),
            pltpu.VMEM((SENSORS, BINS), f32),
        ),
        in_specs=[pl.BlockSpec(memory_space=VMEM)] * 2,
        out_specs=(pl.BlockSpec(memory_space=VMEM),) * 2,
        compiler_params=pltpu.CompilerParams(vmem_limit_bytes=LIMIT),
        cost_estimate=pl.CostEstimate(flops=10**5, bytes_accessed=10**4, transcendentals=0),
        name="cross",
    )(own, far)


def own_kernel(turn_ref, spectra_ref, own_ref, mine_ref):
    shift = lax.rem(SENSORS - 2 * turn_ref[0], SENSORS)
    power = jnp.zeros((SENSORS, BINS), f32)
    for window in range(WIN):
        rows = slice(SENSORS * window, SENSORS * (window + 1))
        block = pltpu.roll(spectra_ref[rows].astype(f32), shift, 0)
        own_ref[rows] = block
        square = block * block
        power = power + (square[:, :BINS] + square[:, BINS:])
    high = power.astype(bf16).astype(f32)
    mine = jnp.concatenate([high, power - high], axis=1)
    for k in range(4):
        mine_ref[k] = jnp.concatenate([mine[2 * k : 2 * k + 2]] * SENSORS, axis=0).astype(bf16)


def own_of(turn, spectra):
    vmem = pl.BlockSpec(memory_space=VMEM)
    return pl.pallas_call(
        own_kernel,
        out_shape=(
            pltpu.VMEM((ROWS, LENGTH), f32),
            pltpu.VMEM((4, 16, LENGTH), bf16),
        ),
        in_specs=[pl.BlockSpec(memory_space=pltpu.MemorySpace.SMEM), vmem],
        out_specs=(vmem, vmem),
        compiler_params=pltpu.CompilerParams(vmem_limit_bytes=LIMIT),
        cost_estimate=pl.CostEstimate(flops=10**5, bytes_accessed=10**4, transcendentals=0),
        name="own",
    )(turn, spectra)


def message_kernel(
    own_ref, third_ref, fourth_ref, s_ref, sp_ref, a_ref, ap_ref, mine_ref, *out_refs
):
    powers = {0: sp_ref[...], 1: ap_ref[...]}
    for slot, far_ref in ((2, third_ref), (3, fourth_ref)):
        collected = []

        def store(real, imag, first, second, third, power):
            put_cross(out_refs, slot * PAIRS, real, imag, first, second, third)
            collected.append(power)

        cross_body(own_ref, far_ref, store)
        powers[slot] = jnp.concatenate(collected, axis=1)
    near = jnp.concatenate(
        [
            jnp.concatenate([powers[0], powers[1]], axis=1),
            jnp.concatenate([powers[2], powers[3]], axis=1),
        ],
        axis=0,
    ).astype(bf16)
    base = CANDS * PAIRS
    for k in range(4):
        out_refs[k][0:PAIRS] = s_ref[k]
        out_refs[k][PAIRS : 2 * PAIRS] = a_ref[k]
        out_refs[k][base : base + 16] = near
        out_refs[k][base + 16 : base + 32] = mine_ref[k]


def messages_of(*parts):
    vmem = pl.BlockSpec(memory_space=VMEM)
    return pl.pallas_call(
        message_kernel,
        out_shape=(pltpu.VMEM((MESSAGE, LENGTH), bf16),) * 4,
        in_specs=[vmem] * 8,
        out_specs=(vmem,) * 4,
        compiler_params=pltpu.CompilerParams(vmem_limit_bytes=LIMIT),
        cost_estimate=pl.CostEstimate(flops=10**5, bytes_accessed=10**4, transcendentals=0),
        name="message",
    )(*parts)


def lag_kernel(tile_ref, blocks_ref, mask_ref, table_ref, *refs):
    got_refs, out_ref, lagged_ref = refs[:4], refs[4], refs[5]
    base = CANDS * PAIRS

    def summed(rows):
        parts = [ref[rows].astype(f32) for ref in got_refs]
        return (parts[0] + parts[1]) + (parts[2] + parts[3])

    def inverse(power):
        return lax.rsqrt(power / (4 * WIN) + 1e-06 * SCALE * SCALE)

    near = inverse(summed(slice(base, base + 16)))
    mine = summed(slice(base + 16, base + 32))
    mine = inverse(mine[:, :BINS] + mine[:, BINS:])
    own = [mine[i : i + 1] for i in range(2)]
    pieces = []
    for slot in range(CANDS):
        row, column = slot // 2, slot % 2
        far = near[SENSORS * row : SENSORS * (row + 1), BINS * column : BINS * (column + 1)]
        cross = summed(slice(slot * PAIRS, (slot + 1) * PAIRS))
        for i in range(2):
            factor = far * own[i]
            factor = jnp.concatenate([factor, factor], axis=1)
            pieces.append(cross[SENSORS * i : SENSORS * (i + 1)] * factor)
    whitened = jnp.concatenate(pieces, axis=0)
    high = whitened.astype(bf16)
    if LAG_PASSES == 1:
        lagged = jnp.dot(high, table_ref[0], preferred_element_type=f32)
    else:
        low = (whitened - high.astype(f32)).astype(bf16)
        both = jnp.concatenate([high, low], axis=0)
        lagged = jnp.dot(both, table_ref[0], preferred_element_type=f32)
        lagged = lagged[: CANDS * PAIRS] + lagged[CANDS * PAIRS :]
        if LAG_PASSES == 3:
            lagged = lagged + jnp.dot(high, table_ref[1], preferred_element_type=f32)
    lagged_ref[...] = lagged.reshape(CANDS, 2, SENSORS, LAGS)
    normaliser = 1.0 / math.sqrt(4 * WIN * BINS)
    tile = tile_ref[0]
    other = 1 - 2 * lax.rem(tile, 2)
    diagonal = lax.broadcasted_iota(jnp.int32, (SENSORS, SENSORS), 0) == (
        lax.broadcasted_iota(jnp.int32, (SENSORS, SENSORS), 1)
    )
    for r in range(4):
        relative = blocks_ref[r] - tile
        slot = jnp.where(
            relative == other,
            0,
            jnp.where(relative == -other, 3, jnp.where(relative == 2 * other, 1, 2)),
        )
        for i in range(2):
            row = mask_ref[i, r : r + 1, :].astype(f32) * normaliser
            column = jnp.sum(jnp.where(diagonal, row, 0.0), axis=1, keepdims=True)
            out_ref[i, r] = lagged_ref[slot, i] * column


def lag_of(tile, blocks, mask, *got):
    smem = pl.BlockSpec(memory_space=pltpu.MemorySpace.SMEM)
    vmem = pl.BlockSpec(memory_space=VMEM)
    table = lag_table()[: max(1, LAG_PASSES - 1)]
    return pl.pallas_call(
        lag_kernel,
        out_shape=jax.ShapeDtypeStruct((2, 4, SENSORS, LAGS), f32),
        in_specs=[smem, smem] + [vmem] * 6,
        out_specs=vmem,
        scratch_shapes=[pltpu.VMEM((CANDS, 2, SENSORS, LAGS), f32)],
        compiler_params=pltpu.CompilerParams(vmem_limit_bytes=LIMIT),
        cost_estimate=pl.CostEstimate(flops=10**5, bytes_accessed=10**4, transcendentals=0),
        name="lag",
    )(tile, blocks, mask, jnp.asarray(table), *got)


def per_device(raw, blocks, mask):
    tiles = lax.axis_size("tile")
    tile = lax.axis_index("tile").astype(jnp.int32).reshape(1)
    turn = lax.axis_index("tm").astype(jnp.int32).reshape(1)

    def ring(block, distances):
        route = [(i, (i + distances[i % 2]) % tiles) for i in range(tiles)]
        return lax.ppermute(block, "tile", route)

    def onward(block, distance):
        groups = lax.axis_size("tm")
        return lax.ppermute(block, "tm", [(i, (i + distance) % groups) for i in range(groups)])

    spectra = spectra_of(raw)
    near = ring(spectra, (1, -1))
    ahead = ring(spectra, (-2, 2))
    behind = ring(spectra, (2, -2))
    own, mine = own_of(turn, spectra)
    s_cross, s_power = cross_of(own, near)
    ahead, s_power = lax.optimization_barrier((ahead, s_power))
    corner = ring(ahead, (1, -1))
    a_cross, a_power = cross_of(own, ahead)
    messages = messages_of(
        own, behind, corner, s_cross, s_power, a_cross, a_power, mine
    )
    got = [messages[0]] + [onward(messages[k], k) for k in (3, 1, 2)]
    return lag_of(tile, blocks, mask, *got)


def solution(mesh):
    placed = (P("tm", "tile", None, None), P("tile"), P("tm", "tile", None))
    return jax.shard_map(
        per_device,
        mesh=mesh,
        in_specs=placed,
        out_specs=P("tm", "tile", None, None),
        check_vma=False,
    )
```

```python
import functools
import math

import jax
import jax.numpy as jnp
import ml_dtypes
import numpy as np
from jax import lax
from jax.experimental import pallas as pl
from jax.experimental.pallas import tpu as pltpu
from jax.sharding import PartitionSpec as P

LAGS = 512
TAPS = 64
DEC = 4
REACH = 2
BINS = 512
LENGTH = 2 * BINS
SENSORS = 8
WIN = 16
ROWS = WIN * SENSORS
LANE = 128
SCALE = 2.0**32
PAIRS = 2 * SENSORS
CANDS = 4
MESSAGE = CANDS * PAIRS + 16 + SENSORS
VMEM = pltpu.MemorySpace.VMEM
CHUNKS = 4
LAG_PASSES = 2
LIMIT = 16 * 1024 * 1024
bf16 = jnp.bfloat16
f32 = jnp.float32


def split_high_low(values):
    high = values.astype(ml_dtypes.bfloat16)
    low = (values - high.astype(np.float32)).astype(ml_dtypes.bfloat16)
    return high, low


def fir_table():
    index = np.arange(TAPS).astype(np.float64)
    centred = (index - (TAPS - 1) / 2.0) / DEC
    taper = 0.5 - 0.5 * np.cos(2.0 * np.pi * (index + 0.5) / TAPS)
    taps = (np.sinc(centred) * taper / DEC).astype(np.float32)
    high, low = split_high_low(taps)
    table = np.zeros((DEC, 2 * LANE, 2 * LANE), ml_dtypes.bfloat16)
    column = np.arange(LANE)
    for phase in range(DEC):
        for offset in range(TAPS // DEC):
            table[phase, column + offset, column] = high[DEC * offset + phase]
            table[phase, column + offset, LANE + column] = low[DEC * offset + phase]
    return table


def dft_table():
    sample = np.arange(LENGTH)[:, None]
    bins = np.arange(BINS)[None, :]
    angle = np.mod(sample * bins, LENGTH).astype(np.float64) * (2.0 * np.pi / LENGTH)
    table = np.concatenate([np.cos(angle), -np.sin(angle)], axis=1).astype(np.float32)
    return (table.astype(ml_dtypes.bfloat16).astype(np.float32) * np.float32(SCALE)).astype(
        ml_dtypes.bfloat16
    )


def lag_table():
    bins = np.arange(BINS)[:, None]
    lag = np.arange(LAGS)[None, :] - LAGS // 2
    angle = np.mod(bins * lag, LENGTH).astype(np.float64) * (2.0 * np.pi / LENGTH)
    weights = np.where(bins == 0, 1.0, 2.0)
    table = np.concatenate([weights * np.cos(angle), -weights * np.sin(angle)], axis=0)
    high, low = split_high_low(table.astype(np.float32))
    return np.stack([high, low])


def spectra_kernel(
    raw_hbm, fir_hbm, dft_hbm, out_ref, raw_ref, fir_ref, dft_ref, wide_ref, sems
):
    def fetch(source, target, index):
        return pltpu.make_async_copy(source, target, sems.at[index])

    windows = raw_ref.shape[0] // CHUNKS
    depth = LENGTH // CHUNKS
    raw_copies = [
        fetch(
            raw_hbm.at[pl.ds(windows * c, windows)], raw_ref.at[pl.ds(windows * c, windows)], c
        )
        for c in range(CHUNKS)
    ]
    fir_copy = fetch(fir_hbm, fir_ref, CHUNKS)
    dft_copies = [
        fetch(
            dft_hbm.at[pl.ds(depth * c, depth)],
            dft_ref.at[pl.ds(depth * c, depth)],
            CHUNKS + 1 + c,
        )
        for c in range(CHUNKS)
    ]
    for copy in raw_copies + [fir_copy] + dft_copies:
        copy.start()
    blocks = LENGTH // LANE
    tail = raw_ref.shape[-1] - LENGTH
    wide_ref[blocks] = jnp.zeros((DEC * ROWS, LANE), f32)
    for c in range(CHUNKS):
        raw_copies[c].wait()
        for row in range(windows * SENSORS * c, windows * SENSORS * (c + 1)):
            place = slice(row * DEC, (row + 1) * DEC)
            values = raw_ref[row // SENSORS, row % SENSORS].astype(f32)
            for k in range(blocks):
                wide_ref[k, place] = values[:, LANE * k : LANE * (k + 1)]
            wide_ref[blocks, place, :tail] = values[:, LENGTH:]
    fir_copy.wait()
    total = jnp.zeros((SENSORS * ROWS, 2 * LANE), f32)
    for phase in range(DEC):
        samples = [
            wide_ref[k, pl.ds(phase, ROWS, stride=DEC), :].astype(bf16) for k in range(blocks + 1)
        ]
        stacked = jnp.concatenate(
            [jnp.concatenate(samples[k : k + 2], axis=1) for k in range(blocks)], axis=0
        )
        total = total + jnp.dot(stacked, fir_ref[phase], preferred_element_type=f32)
    summed = (total[:, :LANE] + total[:, LANE:]).astype(bf16)
    decimated = jnp.concatenate(
        [summed[ROWS * k : ROWS * (k + 1)] for k in range(blocks)], axis=1
    )
    for copy in dft_copies:
        copy.wait()
    spectra = jnp.dot(decimated, dft_ref[...], preferred_element_type=f32)
    out_ref[...] = spectra.astype(bf16)


def in_hbm(array):
    return pltpu.with_memory_space_constraint(array, pltpu.MemorySpace.HBM)


def spectra_of(raw):
    hbm = pl.BlockSpec(memory_space=pltpu.MemorySpace.HBM)
    fir, dft = fir_table(), dft_table()
    return pl.pallas_call(
        spectra_kernel,
        out_shape=pltpu.VMEM((ROWS, LENGTH), bf16),
        in_specs=[hbm, hbm, hbm],
        out_specs=pl.BlockSpec(memory_space=VMEM),
        scratch_shapes=[
            pltpu.VMEM(raw.shape, bf16),
            pltpu.VMEM(fir.shape, bf16),
            pltpu.VMEM(dft.shape, bf16),
            pltpu.VMEM((LENGTH // LANE + 1, DEC * ROWS, LANE), f32),
            pltpu.SemaphoreType.DMA((2 * CHUNKS + 1,)),
        ],
        compiler_params=pltpu.CompilerParams(vmem_limit_bytes=LIMIT),
        cost_estimate=pl.CostEstimate(flops=10**5, bytes_accessed=10**4, transcendentals=0),
        name="spectra",
    )(in_hbm(raw), in_hbm(jnp.asarray(fir)), in_hbm(jnp.asarray(dft)))


def cross_body(own_ref, far_ref, store):
    for tile in range(BINS // LANE):
        real = slice(LANE * tile, LANE * (tile + 1))
        imag = slice(BINS + LANE * tile, BINS + LANE * (tile + 1))

        def step(pair, totals):
            first, second, third, power = totals
            rows = pl.ds(pl.multiple_of(pair * 16, 16), 16)
            own_real = own_ref[rows, real]
            own_imag = own_ref[rows, imag]
            far_real = far_ref[rows, real].astype(f32)
            far_imag = far_ref[rows, imag].astype(f32)
            own_sum = own_real + own_imag
            far_difference = far_real - far_imag
            first, second, third = list(first), list(second), list(third)
            for half in range(2):
                part = slice(SENSORS * half, SENSORS * (half + 1))
                power = power + (far_real[part] * far_real[part] + far_imag[part] * far_imag[part])
                for i in range(SENSORS):
                    row = SENSORS * half + i
                    first[i] = first[i] + own_real[row : row + 1] * far_real[part]
                    second[i] = second[i] + own_imag[row : row + 1] * far_imag[part]
                    third[i] = third[i] + own_sum[row : row + 1] * far_difference[part]
            return tuple(first), tuple(second), tuple(third), power

        zero = jnp.zeros((SENSORS, LANE), f32)
        zeros = (zero,) * SENSORS
        first, second, third, power = lax.fori_loop(
            0, WIN // 2, step, (zeros, zeros, zeros, zero), unroll=True
        )
        store(real, imag, first, second, third, power)


def put_cross(out_refs, base, real, imag, first, second, third):
    for k in range(4):
        pair = [2 * k, 2 * k + 1]
        real_cross = jnp.concatenate([first[i] + second[i] for i in pair], axis=0)
        imag_cross = jnp.concatenate([third[i] - first[i] + second[i] for i in pair], axis=0)
        out_refs[k][base : base + PAIRS, real] = real_cross.astype(bf16)
        out_refs[k][base : base + PAIRS, imag] = imag_cross.astype(bf16)


def cross_kernel(own_ref, far_ref, out_ref, power_ref):
    def store(real, imag, first, second, third, power):
        put_cross([out_ref.at[k] for k in range(4)], 0, real, imag, first, second, third)
        power_ref[:, real] = power

    cross_body(own_ref, far_ref, store)


def cross_of(own, far):
    return pl.pallas_call(
        cross_kernel,
        out_shape=(
            pltpu.VMEM((4, PAIRS, LENGTH), bf16),
            pltpu.VMEM((SENSORS, BINS), f32),
        ),
        in_specs=[pl.BlockSpec(memory_space=VMEM)] * 2,
        out_specs=(pl.BlockSpec(memory_space=VMEM),) * 2,
        compiler_params=pltpu.CompilerParams(vmem_limit_bytes=LIMIT),
        cost_estimate=pl.CostEstimate(flops=10**5, bytes_accessed=10**4, transcendentals=0),
        name="cross",
    )(own, far)


def own_kernel(turn_ref, spectra_ref, own_ref, mine_ref):
    turn = turn_ref[0]
    power = jnp.zeros((SENSORS, BINS), f32)
    sensor = lax.broadcasted_iota(jnp.int32, (SENSORS, LENGTH), 0)
    upper = lax.rem(sensor, 4) >= 2
    odd = lax.rem(turn, 2) == 1
    high = turn >= 2
    for window in range(WIN):
        rows = slice(SENSORS * window, SENSORS * (window + 1))
        block = spectra_ref[rows].astype(f32)
        swapped = jnp.where(upper, pltpu.roll(block, 2, 0), pltpu.roll(block, SENSORS - 2, 0))
        block = jnp.where(odd, swapped, block)
        block = jnp.where(high, pltpu.roll(block, 4, 0), block)
        own_ref[rows] = block
        square = block * block
        power = power + (square[:, :BINS] + square[:, BINS:])
    rounded = power.astype(bf16).astype(f32)
    mine = jnp.concatenate([rounded, power - rounded], axis=1)
    for k in range(4):
        mine_ref[k] = jnp.concatenate([mine[2 * k : 2 * k + 2]] * 4, axis=0)


def own_of(turn, spectra):
    vmem = pl.BlockSpec(memory_space=VMEM)
    return pl.pallas_call(
        own_kernel,
        out_shape=(
            pltpu.VMEM((ROWS, LENGTH), f32),
            pltpu.VMEM((4, SENSORS, LENGTH), f32),
        ),
        in_specs=[pl.BlockSpec(memory_space=pltpu.MemorySpace.SMEM), vmem],
        out_specs=(vmem, vmem),
        compiler_params=pltpu.CompilerParams(vmem_limit_bytes=LIMIT),
        cost_estimate=pl.CostEstimate(flops=10**5, bytes_accessed=10**4, transcendentals=0),
        name="own",
    )(turn, spectra)


def message_kernel(
    own_ref, far_ref, s_ref, sp_ref, a_ref, ap_ref, b_ref, bp_ref, mine_ref, *out_refs
):
    collected = []

    def store(real, imag, first, second, third, power):
        put_cross(out_refs, 3 * PAIRS, real, imag, first, second, third)
        collected.append(power)

    cross_body(own_ref, far_ref, store)
    near = jnp.concatenate(
        [
            jnp.concatenate([sp_ref[...], ap_ref[...]], axis=1),
            jnp.concatenate([bp_ref[...], jnp.concatenate(collected, axis=1)], axis=1),
        ],
        axis=0,
    ).astype(bf16)
    base = CANDS * PAIRS
    for k in range(4):
        out_refs[k][0:PAIRS] = s_ref[k]
        out_refs[k][PAIRS : 2 * PAIRS] = a_ref[k]
        out_refs[k][2 * PAIRS : 3 * PAIRS] = b_ref[k]
        out_refs[k][base : base + 16] = near
        out_refs[k][base + 16 : MESSAGE] = mine_ref[k].astype(bf16)


def messages_of(*parts):
    vmem = pl.BlockSpec(memory_space=VMEM)
    return pl.pallas_call(
        message_kernel,
        out_shape=(pltpu.VMEM((MESSAGE, LENGTH), bf16),) * 4,
        in_specs=[vmem] * len(parts),
        out_specs=(vmem,) * 4,
        compiler_params=pltpu.CompilerParams(vmem_limit_bytes=LIMIT),
        cost_estimate=pl.CostEstimate(flops=10**5, bytes_accessed=10**4, transcendentals=0),
        name="message",
    )(*parts)


def lag_kernel(tile_ref, blocks_ref, mask_ref, table_ref, *refs):
    got_refs, out_ref, lagged_ref = refs[:4], refs[4], refs[5]
    base = CANDS * PAIRS

    def summed(rows):
        parts = [ref[rows].astype(f32) for ref in got_refs]
        return (parts[0] + parts[1]) + (parts[2] + parts[3])

    def inverse(power):
        return lax.rsqrt(power / (4 * WIN) + 1e-06 * SCALE * SCALE)

    near = inverse(summed(slice(base, base + 16)))
    mine = summed(slice(base + 16, MESSAGE))
    mine = inverse(mine[:, :BINS] + mine[:, BINS:])
    own = [mine[i : i + 1] for i in range(2)]
    pieces = []
    for slot in range(CANDS):
        row, column = slot // 2, slot % 2
        far = near[SENSORS * row : SENSORS * (row + 1), BINS * column : BINS * (column + 1)]
        cross = summed(slice(slot * PAIRS, (slot + 1) * PAIRS))
        for i in range(2):
            factor = far * own[i]
            factor = jnp.concatenate([factor, factor], axis=1)
            pieces.append(cross[SENSORS * i : SENSORS * (i + 1)] * factor)
    whitened = jnp.concatenate(pieces, axis=0)
    high = whitened.astype(bf16)
    if LAG_PASSES == 1:
        lagged = jnp.dot(high, table_ref[0], preferred_element_type=f32)
    else:
        low = (whitened - high.astype(f32)).astype(bf16)
        both = jnp.concatenate([high, low], axis=0)
        lagged = jnp.dot(both, table_ref[0], preferred_element_type=f32)
        lagged = lagged[: CANDS * PAIRS] + lagged[CANDS * PAIRS :]
        if LAG_PASSES == 3:
            lagged = lagged + jnp.dot(high, table_ref[1], preferred_element_type=f32)
    lagged_ref[...] = lagged.reshape(CANDS, 2, SENSORS, LAGS)
    normaliser = 1.0 / math.sqrt(4 * WIN * BINS)
    tile = tile_ref[0]
    other = 1 - 2 * lax.rem(tile, 2)
    diagonal = lax.broadcasted_iota(jnp.int32, (SENSORS, SENSORS), 0) == (
        lax.broadcasted_iota(jnp.int32, (SENSORS, SENSORS), 1)
    )
    for r in range(4):
        relative = blocks_ref[r] - tile
        slot = jnp.where(
            relative == other,
            0,
            jnp.where(relative == -other, 3, jnp.where(relative == 2 * other, 1, 2)),
        )
        for i in range(2):
            row = mask_ref[i, r : r + 1, :].astype(f32) * normaliser
            column = jnp.sum(jnp.where(diagonal, row, 0.0), axis=1, keepdims=True)
            out_ref[i, r] = lagged_ref[slot, i] * column


def lag_of(tile, blocks, mask, *got):
    smem = pl.BlockSpec(memory_space=pltpu.MemorySpace.SMEM)
    vmem = pl.BlockSpec(memory_space=VMEM)
    table = lag_table()[: max(1, LAG_PASSES - 1)]
    return pl.pallas_call(
        lag_kernel,
        out_shape=jax.ShapeDtypeStruct((2, 4, SENSORS, LAGS), f32),
        in_specs=[smem, smem] + [vmem] * 6,
        out_specs=vmem,
        scratch_shapes=[pltpu.VMEM((CANDS, 2, SENSORS, LAGS), f32)],
        compiler_params=pltpu.CompilerParams(vmem_limit_bytes=LIMIT),
        cost_estimate=pl.CostEstimate(flops=10**5, bytes_accessed=10**4, transcendentals=0),
        name="lag",
    )(tile, blocks, mask, jnp.asarray(table), *got)


def per_device(raw, blocks, mask):
    tiles = lax.axis_size("tile")
    tile = lax.axis_index("tile").astype(jnp.int32).reshape(1)
    turn = lax.axis_index("tm").astype(jnp.int32).reshape(1)

    def ring(block, distances):
        def target(i):
            there = i + distances[i % 2]
            return there if 0 <= there < tiles else i + 1 - 2 * (i % 2)

        return lax.ppermute(block, "tile", [(i, target(i)) for i in range(tiles)])

    def onward(block, step):
        return lax.ppermute(block, "tm", [(i, i ^ step) for i in range(lax.axis_size("tm"))])

    spectra = spectra_of(raw)
    near = ring(spectra, (1, -1))
    ahead = ring(spectra, (-2, 2))
    behind = ring(spectra, (2, -2))
    own, mine = own_of(turn, spectra)
    s_cross, s_power = cross_of(own, near)
    ahead, s_power = lax.optimization_barrier((ahead, s_power))
    corner = ring(ahead, (1, -1))
    a_cross, a_power = cross_of(own, ahead)
    b_cross, b_power = cross_of(own, behind)
    messages = messages_of(
        own, corner, s_cross, s_power, a_cross, a_power, b_cross, b_power, mine
    )
    got = [messages[0]] + [onward(messages[k], k) for k in (3, 2, 1)]
    return lag_of(tile, blocks, mask, *got)


def solution(mesh):
    placed = (P("tm", "tile", None, None), P("tile"), P("tm", "tile", None))
    return jax.shard_map(
        per_device,
        mesh=mesh,
        in_specs=placed,
        out_specs=P("tm", "tile", None, None),
        check_vma=False,
    )
```

```python
import functools
import math

import jax
import jax.numpy as jnp
import ml_dtypes
import numpy as np
from jax import lax
from jax.experimental import pallas as pl
from jax.experimental.pallas import tpu as pltpu
from jax.sharding import PartitionSpec as P

LAGS = 512
TAPS = 64
DEC = 4
REACH = 2
BINS = 512
HALF = BINS // 2
LENGTH = 2 * BINS
SENSORS = 8
WIN = 16
ROWS = WIN * SENSORS
LANE = 128
REACHED = LANE + 16
SCALE = 2.0**32
PAIRS = 2 * SENSORS
CANDS = 4
MESSAGE = CANDS * PAIRS + 16 + SENSORS
VMEM = pltpu.MemorySpace.VMEM
CHUNKS = 4
LAG_PASSES = 2
LIMIT = 16 * 1024 * 1024
bf16 = jnp.bfloat16
f32 = jnp.float32


def split_high_low(values):
    high = values.astype(ml_dtypes.bfloat16)
    low = (values - high.astype(np.float32)).astype(ml_dtypes.bfloat16)
    return high, low


def fir_table():
    index = np.arange(TAPS).astype(np.float64)
    centred = (index - (TAPS - 1) / 2.0) / DEC
    taper = 0.5 - 0.5 * np.cos(2.0 * np.pi * (index + 0.5) / TAPS)
    taps = (np.sinc(centred) * taper / DEC).astype(np.float32)
    high, low = split_high_low(taps)
    table = np.zeros((DEC, REACHED, 2 * LANE), ml_dtypes.bfloat16)
    sample = np.arange(LANE)
    column = sample // 2 + (sample % 2) * (LANE // 2)
    for phase in range(DEC):
        for offset in range(TAPS // DEC):
            table[phase, sample + offset, column] = high[DEC * offset + phase]
            table[phase, sample + offset, LANE + column] = low[DEC * offset + phase]
    return table


def angles(left, right):
    return np.mod(left * right, LENGTH).astype(np.float64) * (2.0 * np.pi / LENGTH)


def dft_table():
    half = np.arange(LENGTH // 2)[:, None]
    bins = np.arange(HALF)[None, :]
    tables = []
    for parity in range(2):
        angle = angles(2 * half + parity, bins)
        real, imag = np.cos(angle), -np.sin(angle)
        middle = angles(2 * half + parity, BINS // 2)[:, 0]
        imag[:, 0] = -np.sin(middle) if parity else np.cos(middle)
        tables.append(np.concatenate([real, imag], axis=1).astype(np.float32))
    table = np.stack(tables).astype(ml_dtypes.bfloat16).astype(np.float32) * np.float32(SCALE)
    return table.astype(ml_dtypes.bfloat16)


def lag_table():
    bins = np.arange(BINS)
    bins = np.where(bins > HALF, BINS + HALF - bins, bins)[:, None]
    lag = np.arange(LAGS)[None, :] - LAGS // 2
    angle = angles(bins, lag)
    weights = np.where(bins == 0, 1.0, 2.0)
    table = np.concatenate([weights * np.cos(angle), -weights * np.sin(angle)], axis=0)
    high, low = split_high_low(table.astype(np.float32))
    return np.stack([high, low])


def spectra_kernel(
    raw_hbm, fir_hbm, dft_hbm, out_ref, raw_ref, fir_ref, dft_ref, wide_ref, sems
):
    def fetch(source, target, index):
        return pltpu.make_async_copy(source, target, sems.at[index])

    windows = raw_ref.shape[0] // CHUNKS
    parts = 2
    raw_copies = [
        fetch(
            raw_hbm.at[pl.ds(windows * c, windows)], raw_ref.at[pl.ds(windows * c, windows)], c
        )
        for c in range(CHUNKS)
    ]
    fir_copy = fetch(fir_hbm, fir_ref.at[:, pl.ds(0, REACHED)], CHUNKS)
    dft_copies = [
        fetch(
            dft_hbm.at[c],
            dft_ref.at[c],
            CHUNKS + 1 + c,
        )
        for c in range(parts)
    ]
    for copy in raw_copies + [fir_copy] + dft_copies:
        copy.start()
    blocks = LENGTH // LANE
    tail = raw_ref.shape[-1] - LENGTH
    wide_ref[blocks] = jnp.zeros((DEC * ROWS, LANE), f32)
    for c in range(CHUNKS):
        raw_copies[c].wait()
        for row in range(windows * SENSORS * c, windows * SENSORS * (c + 1)):
            place = slice(row * DEC, (row + 1) * DEC)
            values = raw_ref[row // SENSORS, row % SENSORS].astype(f32)
            for k in range(blocks):
                wide_ref[k, place] = values[:, LANE * k : LANE * (k + 1)]
            wide_ref[blocks, place, :tail] = values[:, LENGTH:]
    fir_ref[:, REACHED:] = jnp.zeros((DEC, 2 * LANE - REACHED, 2 * LANE), bf16)
    fir_copy.wait()
    totals = []
    for part in range(2):
        first = blocks // 2 * part
        count = blocks // 2
        columns = []
        for phase in range(DEC):
            pieces = [
                wide_ref[k, pl.ds(phase, ROWS, stride=DEC), :].astype(bf16)
                for k in range(first, first + count + 1)
            ]
            columns.append(
                jnp.concatenate(
                    [jnp.concatenate(pieces[k : k + 2], axis=1) for k in range(count)], axis=0
                )
            )
        totals.append(
            jnp.dot(
                jnp.concatenate(columns, axis=1),
                fir_ref[...].reshape(DEC * 2 * LANE, 2 * LANE),
                preferred_element_type=f32,
            )
        )
    total = jnp.concatenate(totals, axis=0)
    summed = total[:, :LANE] + total[:, LANE:]
    turned = pltpu.roll(summed, LANE // 2, 1)
    lower = lax.broadcasted_iota(jnp.int32, (ROWS, LANE), 1) < LANE // 2
    samples = ([], [])
    for k in range(0, blocks, 2):
        here = slice(ROWS * k, ROWS * (k + 1))
        there = slice(ROWS * (k + 1), ROWS * (k + 2))
        samples[0].append(jnp.where(lower, summed[here], turned[there]))
        samples[1].append(jnp.where(lower, turned[here], summed[there]))
    sums = []
    for parity in range(2):
        decimated = jnp.concatenate(samples[parity], axis=1).astype(bf16)
        dft_copies[parity].wait()
        sums.append(jnp.dot(decimated, dft_ref[parity], preferred_element_type=f32))
    even, odd = sums
    real_sum = even[:, :HALF] + odd[:, :HALF]
    real_difference = even[:, :HALF] - odd[:, :HALF]
    even_imag, odd_imag = even[:, HALF:], odd[:, HALF:]
    first = lax.broadcasted_iota(jnp.int32, (ROWS, HALF), 1) == 0
    out_ref[:, :HALF] = real_sum.astype(bf16)
    out_ref[:, HALF:BINS] = jnp.where(first, even_imag, real_difference).astype(bf16)
    out_ref[:, BINS : BINS + HALF] = jnp.where(first, 0.0, even_imag + odd_imag).astype(bf16)
    out_ref[:, BINS + HALF :] = jnp.where(first, odd_imag, odd_imag - even_imag).astype(bf16)


def in_hbm(array):
    return pltpu.with_memory_space_constraint(array, pltpu.MemorySpace.HBM)


def spectra_of(raw):
    hbm = pl.BlockSpec(memory_space=pltpu.MemorySpace.HBM)
    fir, dft = fir_table(), dft_table()
    return pl.pallas_call(
        spectra_kernel,
        out_shape=pltpu.VMEM((ROWS, LENGTH), bf16),
        in_specs=[hbm, hbm, hbm],
        out_specs=pl.BlockSpec(memory_space=VMEM),
        scratch_shapes=[
            pltpu.VMEM(raw.shape, bf16),
            pltpu.VMEM((DEC, 2 * LANE, 2 * LANE), bf16),
            pltpu.VMEM(dft.shape, bf16),
            pltpu.VMEM((LENGTH // LANE + 1, DEC * ROWS, LANE), f32),
            pltpu.SemaphoreType.DMA((2 * CHUNKS + 1,)),
        ],
        compiler_params=pltpu.CompilerParams(vmem_limit_bytes=LIMIT),
        cost_estimate=pl.CostEstimate(flops=10**5, bytes_accessed=10**4, transcendentals=0),
        name="spectra",
    )(in_hbm(raw), in_hbm(jnp.asarray(fir)), in_hbm(jnp.asarray(dft)))


def cross_body(own_ref, far_ref, store):
    for tile in range(BINS // LANE):
        real = slice(LANE * tile, LANE * (tile + 1))
        imag = slice(BINS + LANE * tile, BINS + LANE * (tile + 1))

        def step(pair, totals):
            first, second, third, power = totals
            rows = pl.ds(pl.multiple_of(pair * 16, 16), 16)
            own_real = own_ref[rows, real]
            own_imag = own_ref[rows, imag]
            far_real = far_ref[rows, real].astype(f32)
            far_imag = far_ref[rows, imag].astype(f32)
            own_sum = own_real + own_imag
            far_difference = far_real - far_imag
            first, second, third = list(first), list(second), list(third)
            for half in range(2):
                part = slice(SENSORS * half, SENSORS * (half + 1))
                power = power + (far_real[part] * far_real[part] + far_imag[part] * far_imag[part])
                for i in range(SENSORS):
                    row = SENSORS * half + i
                    first[i] = first[i] + own_real[row : row + 1] * far_real[part]
                    second[i] = second[i] + own_imag[row : row + 1] * far_imag[part]
                    third[i] = third[i] + own_sum[row : row + 1] * far_difference[part]
            return tuple(first), tuple(second), tuple(third), power

        zero = jnp.zeros((SENSORS, LANE), f32)
        zeros = (zero,) * SENSORS
        first, second, third, power = lax.fori_loop(
            0, WIN // 2, step, (zeros, zeros, zeros, zero), unroll=True
        )
        store(real, imag, first, second, third, power)


def put_cross(out_refs, base, real, imag, first, second, third):
    for k in range(4):
        pair = [2 * k, 2 * k + 1]
        real_cross = jnp.concatenate([first[i] + second[i] for i in pair], axis=0)
        imag_cross = jnp.concatenate([third[i] - first[i] + second[i] for i in pair], axis=0)
        out_refs[k][base : base + PAIRS, real] = real_cross.astype(bf16)
        out_refs[k][base : base + PAIRS, imag] = imag_cross.astype(bf16)


def cross_kernel(own_ref, far_ref, out_ref, power_ref):
    def store(real, imag, first, second, third, power):
        put_cross([out_ref.at[k] for k in range(4)], 0, real, imag, first, second, third)
        power_ref[:, real] = power

    cross_body(own_ref, far_ref, store)


def cross_of(own, far):
    return pl.pallas_call(
        cross_kernel,
        out_shape=(
            pltpu.VMEM((4, PAIRS, LENGTH), bf16),
            pltpu.VMEM((SENSORS, BINS), f32),
        ),
        in_specs=[pl.BlockSpec(memory_space=VMEM)] * 2,
        out_specs=(pl.BlockSpec(memory_space=VMEM),) * 2,
        compiler_params=pltpu.CompilerParams(vmem_limit_bytes=LIMIT),
        cost_estimate=pl.CostEstimate(flops=10**5, bytes_accessed=10**4, transcendentals=0),
        name="cross",
    )(own, far)


def own_kernel(turn_ref, spectra_ref, own_ref, mine_ref):
    turn = turn_ref[0]
    power = jnp.zeros((SENSORS, BINS), f32)
    sensor = lax.broadcasted_iota(jnp.int32, (SENSORS, LENGTH), 0)
    upper = lax.rem(sensor, 4) >= 2
    odd = lax.rem(turn, 2) == 1
    high = turn >= 2
    for window in range(WIN):
        rows = slice(SENSORS * window, SENSORS * (window + 1))
        block = spectra_ref[rows].astype(f32)
        swapped = jnp.where(upper, pltpu.roll(block, 2, 0), pltpu.roll(block, SENSORS - 2, 0))
        block = jnp.where(odd, swapped, block)
        block = jnp.where(high, pltpu.roll(block, 4, 0), block)
        own_ref[rows] = block
        square = block * block
        power = power + (square[:, :BINS] + square[:, BINS:])
    rounded = power.astype(bf16).astype(f32)
    mine = jnp.concatenate([rounded, power - rounded], axis=1)
    for k in range(4):
        mine_ref[k] = jnp.concatenate([mine[2 * k : 2 * k + 2]] * 4, axis=0)


def own_of(turn, spectra):
    vmem = pl.BlockSpec(memory_space=VMEM)
    return pl.pallas_call(
        own_kernel,
        out_shape=(
            pltpu.VMEM((ROWS, LENGTH), f32),
            pltpu.VMEM((4, SENSORS, LENGTH), f32),
        ),
        in_specs=[pl.BlockSpec(memory_space=pltpu.MemorySpace.SMEM), vmem],
        out_specs=(vmem, vmem),
        compiler_params=pltpu.CompilerParams(vmem_limit_bytes=LIMIT),
        cost_estimate=pl.CostEstimate(flops=10**5, bytes_accessed=10**4, transcendentals=0),
        name="own",
    )(turn, spectra)


def message_kernel(
    own_ref, far_ref, s_ref, sp_ref, a_ref, ap_ref, b_ref, bp_ref, mine_ref, *out_refs
):
    collected = []

    def store(real, imag, first, second, third, power):
        put_cross(out_refs, 3 * PAIRS, real, imag, first, second, third)
        collected.append(power)

    cross_body(own_ref, far_ref, store)
    near = jnp.concatenate(
        [
            jnp.concatenate([sp_ref[...], ap_ref[...]], axis=1),
            jnp.concatenate([bp_ref[...], jnp.concatenate(collected, axis=1)], axis=1),
        ],
        axis=0,
    ).astype(bf16)
    base = CANDS * PAIRS
    for k in range(4):
        out_refs[k][0:PAIRS] = s_ref[k]
        out_refs[k][PAIRS : 2 * PAIRS] = a_ref[k]
        out_refs[k][2 * PAIRS : 3 * PAIRS] = b_ref[k]
        out_refs[k][base : base + 16] = near
        out_refs[k][base + 16 : MESSAGE] = mine_ref[k].astype(bf16)


def messages_of(*parts):
    vmem = pl.BlockSpec(memory_space=VMEM)
    return pl.pallas_call(
        message_kernel,
        out_shape=(pltpu.VMEM((MESSAGE, LENGTH), bf16),) * 4,
        in_specs=[vmem] * len(parts),
        out_specs=(vmem,) * 4,
        compiler_params=pltpu.CompilerParams(vmem_limit_bytes=LIMIT),
        cost_estimate=pl.CostEstimate(flops=10**5, bytes_accessed=10**4, transcendentals=0),
        name="message",
    )(*parts)


def lag_kernel(tile_ref, blocks_ref, mask_ref, table_ref, *refs):
    got_refs, out_ref, lagged_ref = refs[:4], refs[4], refs[5]
    base = CANDS * PAIRS

    def summed(rows):
        parts = [ref[rows].astype(f32) for ref in got_refs]
        return (parts[0] + parts[1]) + (parts[2] + parts[3])

    def inverse(power):
        return lax.rsqrt(power / (4 * WIN) + 1e-06 * SCALE * SCALE)

    near = inverse(summed(slice(base, base + 16)))
    mine = summed(slice(base + 16, MESSAGE))
    mine = inverse(mine[:, :BINS] + mine[:, BINS:])
    own = [mine[i : i + 1] for i in range(2)]
    pieces = []
    for slot in range(CANDS):
        row, column = slot // 2, slot % 2
        far = near[SENSORS * row : SENSORS * (row + 1), BINS * column : BINS * (column + 1)]
        cross = summed(slice(slot * PAIRS, (slot + 1) * PAIRS))
        for i in range(2):
            factor = far * own[i]
            factor = jnp.concatenate([factor, factor], axis=1)
            pieces.append(cross[SENSORS * i : SENSORS * (i + 1)] * factor)
    whitened = jnp.concatenate(pieces, axis=0)
    high = whitened.astype(bf16)
    if LAG_PASSES == 1:
        lagged = jnp.dot(high, table_ref[0], preferred_element_type=f32)
    else:
        low = (whitened - high.astype(f32)).astype(bf16)
        both = jnp.concatenate([high, low], axis=0)
        lagged = jnp.dot(both, table_ref[0], preferred_element_type=f32)
        lagged = lagged[: CANDS * PAIRS] + lagged[CANDS * PAIRS :]
        if LAG_PASSES == 3:
            lagged = lagged + jnp.dot(high, table_ref[1], preferred_element_type=f32)
    lagged_ref[...] = lagged.reshape(CANDS, 2, SENSORS, LAGS)
    normaliser = 1.0 / math.sqrt(4 * WIN * BINS)
    tile = tile_ref[0]
    other = 1 - 2 * lax.rem(tile, 2)
    diagonal = lax.broadcasted_iota(jnp.int32, (SENSORS, SENSORS), 0) == (
        lax.broadcasted_iota(jnp.int32, (SENSORS, SENSORS), 1)
    )
    for r in range(4):
        relative = blocks_ref[r] - tile
        slot = jnp.where(
            relative == other,
            0,
            jnp.where(relative == -other, 3, jnp.where(relative == 2 * other, 1, 2)),
        )
        for i in range(2):
            row = mask_ref[i, r : r + 1, :].astype(f32) * normaliser
            column = jnp.sum(jnp.where(diagonal, row, 0.0), axis=1, keepdims=True)
            out_ref[i, r] = lagged_ref[slot, i] * column


def lag_of(tile, blocks, mask, *got):
    smem = pl.BlockSpec(memory_space=pltpu.MemorySpace.SMEM)
    vmem = pl.BlockSpec(memory_space=VMEM)
    table = lag_table()[: max(1, LAG_PASSES - 1)]
    return pl.pallas_call(
        lag_kernel,
        out_shape=jax.ShapeDtypeStruct((2, 4, SENSORS, LAGS), f32),
        in_specs=[smem, smem] + [vmem] * 6,
        out_specs=vmem,
        scratch_shapes=[pltpu.VMEM((CANDS, 2, SENSORS, LAGS), f32)],
        compiler_params=pltpu.CompilerParams(vmem_limit_bytes=LIMIT),
        cost_estimate=pl.CostEstimate(flops=10**5, bytes_accessed=10**4, transcendentals=0),
        name="lag",
    )(tile, blocks, mask, jnp.asarray(table), *got)


def per_device(raw, blocks, mask):
    tiles = lax.axis_size("tile")
    tile = lax.axis_index("tile").astype(jnp.int32).reshape(1)
    turn = lax.axis_index("tm").astype(jnp.int32).reshape(1)

    def ring(block, distances):
        def target(i):
            there = i + distances[i % 2]
            return there if 0 <= there < tiles else i + 1 - 2 * (i % 2)

        return lax.ppermute(block, "tile", [(i, target(i)) for i in range(tiles)])

    def onward(block, step):
        return lax.ppermute(block, "tm", [(i, i ^ step) for i in range(lax.axis_size("tm"))])

    spectra = spectra_of(raw)
    near = ring(spectra, (1, -1))
    ahead = ring(spectra, (-2, 2))
    behind = ring(spectra, (2, -2))
    own, mine = own_of(turn, spectra)
    s_cross, s_power = cross_of(own, near)
    ahead, s_power = lax.optimization_barrier((ahead, s_power))
    corner = ring(ahead, (1, -1))
    a_cross, a_power = cross_of(own, ahead)
    b_cross, b_power = cross_of(own, behind)
    messages = messages_of(
        own, corner, s_cross, s_power, a_cross, a_power, b_cross, b_power, mine
    )
    got = [messages[0]] + [onward(messages[k], k) for k in (3, 2, 1)]
    return lag_of(tile, blocks, mask, *got)


def solution(mesh):
    placed = (P("tm", "tile", None, None), P("tile"), P("tm", "tile", None))
    return jax.shard_map(
        per_device,
        mesh=mesh,
        in_specs=placed,
        out_specs=P("tm", "tile", None, None),
        check_vma=False,
    )
```

```python
import functools
import math

import jax
import jax.numpy as jnp
import ml_dtypes
import numpy as np
from jax import lax
from jax.experimental import pallas as pl
from jax.experimental.pallas import tpu as pltpu
from jax.sharding import PartitionSpec as P

LAGS = 512
TAPS = 64
DEC = 4
REACH = 2
BINS = 512
HALF = BINS // 2
LENGTH = 2 * BINS
SENSORS = 8
WIN = 16
ROWS = WIN * SENSORS
LANE = 128
REACHED = LANE + 16
SCALE = 2.0**32
PAIRS = 2 * SENSORS
CANDS = 4
MESSAGE = CANDS * PAIRS + 16 + SENSORS
VMEM = pltpu.MemorySpace.VMEM
CHUNKS = 4
LIMIT = 16 * 1024 * 1024
bf16 = jnp.bfloat16
f32 = jnp.float32


def split_high_low(values):
    high = values.astype(ml_dtypes.bfloat16)
    low = (values - high.astype(np.float32)).astype(ml_dtypes.bfloat16)
    return high, low


def fir_table():
    index = np.arange(TAPS).astype(np.float64)
    centred = (index - (TAPS - 1) / 2.0) / DEC
    taper = 0.5 - 0.5 * np.cos(2.0 * np.pi * (index + 0.5) / TAPS)
    taps = (np.sinc(centred) * taper / DEC).astype(np.float32)
    high, low = split_high_low(taps)
    table = np.zeros((DEC, REACHED, 2 * LANE), ml_dtypes.bfloat16)
    sample = np.arange(LANE)
    column = sample // 2 + (sample % 2) * (LANE // 2)
    for phase in range(DEC):
        for offset in range(TAPS // DEC):
            table[phase, sample + offset, column] = high[DEC * offset + phase]
            table[phase, sample + offset, LANE + column] = low[DEC * offset + phase]
    return table


def angles(left, right):
    return np.mod(left * right, LENGTH).astype(np.float64) * (2.0 * np.pi / LENGTH)


def dft_table():
    half = np.arange(LENGTH // 2)[:, None]
    bins = np.arange(HALF)[None, :]
    tables = []
    for parity in range(2):
        angle = angles(2 * half + parity, bins)
        real, imag = np.cos(angle), -np.sin(angle)
        middle = angles(2 * half + parity, BINS // 2)[:, 0]
        imag[:, 0] = -np.sin(middle) if parity else np.cos(middle)
        tables.append(np.concatenate([real, imag], axis=1).astype(np.float32))
    table = np.stack(tables).astype(ml_dtypes.bfloat16).astype(np.float32) * np.float32(SCALE)
    return table.astype(ml_dtypes.bfloat16)


def lag_table():
    bins = np.arange(BINS)
    bins = np.where(bins > HALF, BINS + HALF - bins, bins)[:, None]
    lag = np.arange(LAGS)[None, :] - LAGS // 2
    angle = angles(bins, lag)
    weights = np.where(bins == 0, 1.0, 2.0)
    table = np.concatenate([weights * np.cos(angle), -weights * np.sin(angle)], axis=0)
    return table.astype(np.float32).astype(ml_dtypes.bfloat16)


def spectra_kernel(
    raw_hbm, fir_hbm, dft_hbm, out_ref, raw_ref, fir_ref, dft_ref, wide_ref, sems
):
    def fetch(source, target, index):
        return pltpu.make_async_copy(source, target, sems.at[index])

    windows = raw_ref.shape[0] // CHUNKS
    parts = 2
    raw_copies = [
        fetch(
            raw_hbm.at[pl.ds(windows * c, windows)], raw_ref.at[pl.ds(windows * c, windows)], c
        )
        for c in range(CHUNKS)
    ]
    fir_copy = fetch(fir_hbm, fir_ref.at[:, pl.ds(0, REACHED)], CHUNKS)
    dft_copies = [
        fetch(
            dft_hbm.at[c],
            dft_ref.at[c],
            CHUNKS + 1 + c,
        )
        for c in range(parts)
    ]
    for copy in raw_copies + [fir_copy] + dft_copies:
        copy.start()
    blocks = LENGTH // LANE
    tail = raw_ref.shape[-1] - LENGTH
    wide_ref[blocks] = jnp.zeros((DEC * ROWS, LANE), f32)
    for c in range(CHUNKS):
        raw_copies[c].wait()
        for row in range(windows * SENSORS * c, windows * SENSORS * (c + 1)):
            place = slice(row * DEC, (row + 1) * DEC)
            values = raw_ref[row // SENSORS, row % SENSORS].astype(f32)
            for k in range(blocks):
                wide_ref[k, place] = values[:, LANE * k : LANE * (k + 1)]
            wide_ref[blocks, place, :tail] = values[:, LENGTH:]
    fir_ref[:, REACHED:] = jnp.zeros((DEC, 2 * LANE - REACHED, 2 * LANE), bf16)
    fir_copy.wait()
    totals = []
    for part in range(2):
        first = blocks // 2 * part
        count = blocks // 2
        columns = []
        for phase in range(DEC):
            pieces = [
                wide_ref[k, pl.ds(phase, ROWS, stride=DEC), :].astype(bf16)
                for k in range(first, first + count + 1)
            ]
            columns.append(
                jnp.concatenate(
                    [jnp.concatenate(pieces[k : k + 2], axis=1) for k in range(count)], axis=0
                )
            )
        totals.append(
            jnp.dot(
                jnp.concatenate(columns, axis=1),
                fir_ref[...].reshape(DEC * 2 * LANE, 2 * LANE),
                preferred_element_type=f32,
            )
        )
    total = jnp.concatenate(totals, axis=0)
    summed = total[:, :LANE] + total[:, LANE:]
    turned = pltpu.roll(summed, LANE // 2, 1)
    lower = lax.broadcasted_iota(jnp.int32, (ROWS, LANE), 1) < LANE // 2
    samples = ([], [])
    for k in range(0, blocks, 2):
        here = slice(ROWS * k, ROWS * (k + 1))
        there = slice(ROWS * (k + 1), ROWS * (k + 2))
        samples[0].append(jnp.where(lower, summed[here], turned[there]))
        samples[1].append(jnp.where(lower, turned[here], summed[there]))
    sums = []
    for parity in range(2):
        decimated = jnp.concatenate(samples[parity], axis=1).astype(bf16)
        dft_copies[parity].wait()
        sums.append(jnp.dot(decimated, dft_ref[parity], preferred_element_type=f32))
    even, odd = sums
    real_sum = even[:, :HALF] + odd[:, :HALF]
    real_difference = even[:, :HALF] - odd[:, :HALF]
    even_imag, odd_imag = even[:, HALF:], odd[:, HALF:]
    first = lax.broadcasted_iota(jnp.int32, (ROWS, HALF), 1) == 0
    out_ref[:, :HALF] = real_sum.astype(bf16)
    out_ref[:, HALF:BINS] = jnp.where(first, even_imag, real_difference).astype(bf16)
    out_ref[:, BINS : BINS + HALF] = jnp.where(first, 0.0, even_imag + odd_imag).astype(bf16)
    out_ref[:, BINS + HALF :] = jnp.where(first, odd_imag, odd_imag - even_imag).astype(bf16)


def in_hbm(array):
    return pltpu.with_memory_space_constraint(array, pltpu.MemorySpace.HBM)


def spectra_of(raw):
    hbm = pl.BlockSpec(memory_space=pltpu.MemorySpace.HBM)
    fir, dft = fir_table(), dft_table()
    return pl.pallas_call(
        spectra_kernel,
        out_shape=pltpu.VMEM((ROWS, LENGTH), bf16),
        in_specs=[hbm, hbm, hbm],
        out_specs=pl.BlockSpec(memory_space=VMEM),
        scratch_shapes=[
            pltpu.VMEM(raw.shape, bf16),
            pltpu.VMEM((DEC, 2 * LANE, 2 * LANE), bf16),
            pltpu.VMEM(dft.shape, bf16),
            pltpu.VMEM((LENGTH // LANE + 1, DEC * ROWS, LANE), f32),
            pltpu.SemaphoreType.DMA((2 * CHUNKS + 1,)),
        ],
        compiler_params=pltpu.CompilerParams(vmem_limit_bytes=LIMIT),
        cost_estimate=pl.CostEstimate(flops=10**5, bytes_accessed=10**4, transcendentals=0),
        name="spectra",
    )(in_hbm(raw), in_hbm(jnp.asarray(fir)), in_hbm(jnp.asarray(dft)))


def cross_body(own_ref, far_ref, store):
    for tile in range(BINS // LANE):
        real = slice(LANE * tile, LANE * (tile + 1))
        imag = slice(BINS + LANE * tile, BINS + LANE * (tile + 1))
        both = slice(LENGTH + LANE * tile, LENGTH + LANE * (tile + 1))

        def step(pair, totals):
            first, second, third, power = totals
            rows = pl.ds(pl.multiple_of(pair * 16, 16), 16)
            far_real = far_ref[rows, real].astype(f32)
            far_imag = far_ref[rows, imag].astype(f32)
            far_difference = far_real - far_imag
            first, second, third = list(first), list(second), list(third)
            for half in range(2):
                part = slice(SENSORS * half, SENSORS * (half + 1))
                power = power + (far_real[part] * far_real[part] + far_imag[part] * far_imag[part])
                for i in range(SENSORS):
                    row = pl.ds(pair * 16 + SENSORS * half + i, 1)
                    first[i] = first[i] + own_ref[row, real] * far_real[part]
                    second[i] = second[i] + own_ref[row, imag] * far_imag[part]
                    third[i] = third[i] + own_ref[row, both] * far_difference[part]
            return tuple(first), tuple(second), tuple(third), power

        zero = jnp.zeros((SENSORS, LANE), f32)
        zeros = (zero,) * SENSORS
        first, second, third, power = lax.fori_loop(
            0, WIN // 2, step, (zeros, zeros, zeros, zero), unroll=True
        )
        store(real, imag, first, second, third, power)


def put_cross(out_refs, base, real, imag, first, second, third):
    for k in range(4):
        pair = [2 * k, 2 * k + 1]
        real_cross = jnp.concatenate([first[i] + second[i] for i in pair], axis=0)
        imag_cross = jnp.concatenate([third[i] - first[i] + second[i] for i in pair], axis=0)
        out_refs[k][base : base + PAIRS, real] = real_cross.astype(bf16)
        out_refs[k][base : base + PAIRS, imag] = imag_cross.astype(bf16)


def cross_kernel(own_ref, far_ref, out_ref, power_ref):
    def store(real, imag, first, second, third, power):
        put_cross([out_ref.at[k] for k in range(4)], 0, real, imag, first, second, third)
        power_ref[:, real] = power

    cross_body(own_ref, far_ref, store)


def cross_of(own, far):
    return pl.pallas_call(
        cross_kernel,
        out_shape=(
            pltpu.VMEM((4, PAIRS, LENGTH), bf16),
            pltpu.VMEM((SENSORS, BINS), f32),
        ),
        in_specs=[pl.BlockSpec(memory_space=VMEM)] * 2,
        out_specs=(pl.BlockSpec(memory_space=VMEM),) * 2,
        compiler_params=pltpu.CompilerParams(vmem_limit_bytes=LIMIT),
        cost_estimate=pl.CostEstimate(flops=10**5, bytes_accessed=10**4, transcendentals=0),
        name="cross",
    )(own, far)


def own_kernel(turn_ref, spectra_ref, own_ref, mine_ref):
    turn = turn_ref[0]
    power = jnp.zeros((SENSORS, BINS), f32)
    sensor = lax.broadcasted_iota(jnp.int32, (SENSORS, LENGTH), 0)
    upper = lax.rem(sensor, 4) >= 2
    odd = lax.rem(turn, 2) == 1
    high = turn >= 2
    for window in range(WIN):
        rows = slice(SENSORS * window, SENSORS * (window + 1))
        block = spectra_ref[rows].astype(f32)
        swapped = jnp.where(upper, pltpu.roll(block, 2, 0), pltpu.roll(block, SENSORS - 2, 0))
        block = jnp.where(odd, swapped, block)
        block = jnp.where(high, pltpu.roll(block, 4, 0), block)
        own_ref[rows, :LENGTH] = block
        own_ref[rows, LENGTH:] = block[:, :BINS] + block[:, BINS:]
        square = block * block
        power = power + (square[:, :BINS] + square[:, BINS:])
    rounded = power.astype(bf16).astype(f32)
    mine = jnp.concatenate([rounded, power - rounded], axis=1)
    for k in range(4):
        mine_ref[k] = jnp.concatenate([mine[2 * k : 2 * k + 2]] * 4, axis=0)


def own_of(turn, spectra):
    vmem = pl.BlockSpec(memory_space=VMEM)
    return pl.pallas_call(
        own_kernel,
        out_shape=(
            pltpu.VMEM((ROWS, LENGTH + BINS), f32),
            pltpu.VMEM((4, SENSORS, LENGTH), f32),
        ),
        in_specs=[pl.BlockSpec(memory_space=pltpu.MemorySpace.SMEM), vmem],
        out_specs=(vmem, vmem),
        compiler_params=pltpu.CompilerParams(vmem_limit_bytes=LIMIT),
        cost_estimate=pl.CostEstimate(flops=10**5, bytes_accessed=10**4, transcendentals=0),
        name="own",
    )(turn, spectra)


def message_kernel(
    own_ref, far_ref, s_ref, sp_ref, a_ref, ap_ref, b_ref, bp_ref, mine_ref, *out_refs
):
    collected = []

    def store(real, imag, first, second, third, power):
        put_cross(out_refs, 3 * PAIRS, real, imag, first, second, third)
        collected.append(power)

    cross_body(own_ref, far_ref, store)
    near = jnp.concatenate(
        [
            jnp.concatenate([sp_ref[...], ap_ref[...]], axis=1),
            jnp.concatenate([bp_ref[...], jnp.concatenate(collected, axis=1)], axis=1),
        ],
        axis=0,
    ).astype(bf16)
    base = CANDS * PAIRS
    for k in range(4):
        out_refs[k][0:PAIRS] = s_ref[k]
        out_refs[k][PAIRS : 2 * PAIRS] = a_ref[k]
        out_refs[k][2 * PAIRS : 3 * PAIRS] = b_ref[k]
        out_refs[k][base : base + 16] = near
        out_refs[k][base + 16 : MESSAGE] = mine_ref[k].astype(bf16)


def messages_of(*parts):
    vmem = pl.BlockSpec(memory_space=VMEM)
    return pl.pallas_call(
        message_kernel,
        out_shape=(pltpu.VMEM((MESSAGE, LENGTH), bf16),) * 4,
        in_specs=[vmem] * len(parts),
        out_specs=(vmem,) * 4,
        compiler_params=pltpu.CompilerParams(vmem_limit_bytes=LIMIT),
        cost_estimate=pl.CostEstimate(flops=10**5, bytes_accessed=10**4, transcendentals=0),
        name="message",
    )(*parts)


def lag_kernel(tile_ref, blocks_ref, mask_ref, table_ref, *refs):
    got_refs, out_ref, lagged_ref = refs[:4], refs[4], refs[5]
    base = CANDS * PAIRS

    def summed(rows):
        parts = [ref[rows].astype(f32) for ref in got_refs]
        return (parts[0] + parts[1]) + (parts[2] + parts[3])

    def inverse(power):
        return lax.rsqrt(power / (4 * WIN) + 1e-06 * SCALE * SCALE)

    near = inverse(summed(slice(base, base + 16)))
    mine = summed(slice(base + 16, MESSAGE))
    mine = inverse(mine[:, :BINS] + mine[:, BINS:])
    own = [mine[i : i + 1] for i in range(2)]
    pieces = []
    for slot in range(CANDS):
        row, column = slot // 2, slot % 2
        far = near[SENSORS * row : SENSORS * (row + 1), BINS * column : BINS * (column + 1)]
        cross = summed(slice(slot * PAIRS, (slot + 1) * PAIRS))
        for i in range(2):
            factor = far * own[i]
            factor = jnp.concatenate([factor, factor], axis=1)
            pieces.append(cross[SENSORS * i : SENSORS * (i + 1)] * factor)
    whitened = jnp.concatenate(pieces, axis=0)
    high = whitened.astype(bf16)
    low = (whitened - high.astype(f32)).astype(bf16)
    both = jnp.concatenate([high, low], axis=0)
    lagged = jnp.dot(both, table_ref[...], preferred_element_type=f32)
    lagged = lagged[: CANDS * PAIRS] + lagged[CANDS * PAIRS :]
    lagged_ref[...] = lagged.reshape(CANDS, 2, SENSORS, LAGS)
    normaliser = 1.0 / math.sqrt(4 * WIN * BINS)
    tile = tile_ref[0]
    other = 1 - 2 * lax.rem(tile, 2)
    diagonal = lax.broadcasted_iota(jnp.int32, (SENSORS, SENSORS), 0) == (
        lax.broadcasted_iota(jnp.int32, (SENSORS, SENSORS), 1)
    )
    for r in range(4):
        relative = blocks_ref[r] - tile
        slot = jnp.where(
            relative == other,
            0,
            jnp.where(relative == -other, 3, jnp.where(relative == 2 * other, 1, 2)),
        )
        for i in range(2):
            row = mask_ref[i, r : r + 1, :].astype(f32) * normaliser
            column = jnp.sum(jnp.where(diagonal, row, 0.0), axis=1, keepdims=True)
            out_ref[i, r] = lagged_ref[slot, i] * column


def lag_of(tile, blocks, mask, *got):
    smem = pl.BlockSpec(memory_space=pltpu.MemorySpace.SMEM)
    vmem = pl.BlockSpec(memory_space=VMEM)
    table = lag_table()
    return pl.pallas_call(
        lag_kernel,
        out_shape=jax.ShapeDtypeStruct((2, 4, SENSORS, LAGS), f32),
        in_specs=[smem, smem] + [vmem] * 6,
        out_specs=vmem,
        scratch_shapes=[pltpu.VMEM((CANDS, 2, SENSORS, LAGS), f32)],
        compiler_params=pltpu.CompilerParams(vmem_limit_bytes=LIMIT),
        cost_estimate=pl.CostEstimate(flops=10**5, bytes_accessed=10**4, transcendentals=0),
        name="lag",
    )(tile, blocks, mask, jnp.asarray(table), *got)


def per_device(raw, blocks, mask):
    tiles = lax.axis_size("tile")
    tile = lax.axis_index("tile").astype(jnp.int32).reshape(1)
    turn = lax.axis_index("tm").astype(jnp.int32).reshape(1)

    def ring(block, distances):
        def target(i):
            there = i + distances[i % 2]
            return there if 0 <= there < tiles else i + 1 - 2 * (i % 2)

        return lax.ppermute(block, "tile", [(i, target(i)) for i in range(tiles)])

    def onward(block, step):
        return lax.ppermute(block, "tm", [(i, i ^ step) for i in range(lax.axis_size("tm"))])

    spectra = spectra_of(raw)
    near = ring(spectra, (1, -1))
    ahead = ring(spectra, (-2, 2))
    behind = ring(spectra, (2, -2))
    own, mine = own_of(turn, spectra)
    s_cross, s_power = cross_of(own, near)
    ahead, s_power = lax.optimization_barrier((ahead, s_power))
    corner = ring(ahead, (1, -1))
    a_cross, a_power = cross_of(own, ahead)
    b_cross, b_power = cross_of(own, behind)
    messages = messages_of(
        own, corner, s_cross, s_power, a_cross, a_power, b_cross, b_power, mine
    )
    got = [messages[0]] + [onward(messages[k], k) for k in (2, 1, 3)]
    return lag_of(tile, blocks, mask, *got)


def solution(mesh):
    placed = (P("tm", "tile", None, None), P("tile"), P("tm", "tile", None))
    return jax.shard_map(
        per_device,
        mesh=mesh,
        in_specs=placed,
        out_specs=P("tm", "tile", None, None),
        check_vma=False,
    )
```

```python
import functools
import math

import jax
import jax.numpy as jnp
import ml_dtypes
import numpy as np
from jax import lax
from jax.experimental import pallas as pl
from jax.experimental.pallas import tpu as pltpu
from jax.sharding import PartitionSpec as P

LAGS = 512
TAPS = 64
DEC = 4
REACH = 2
BINS = 512
HALF = BINS // 2
LENGTH = 2 * BINS
SENSORS = 8
WIN = 16
ROWS = WIN * SENSORS
LANE = 128
REACHED = LANE + 16
SCALE = 2.0**32
PAIRS = 2 * SENSORS
CANDS = 4
MESSAGE = CANDS * PAIRS + 16 + SENSORS
VMEM = pltpu.MemorySpace.VMEM
CHUNKS = 4
LIMIT = 16 * 1024 * 1024
bf16 = jnp.bfloat16
f32 = jnp.float32


def split_high_low(values):
    high = values.astype(ml_dtypes.bfloat16)
    low = (values - high.astype(np.float32)).astype(ml_dtypes.bfloat16)
    return high, low


def fir_table():
    index = np.arange(TAPS).astype(np.float64)
    centred = (index - (TAPS - 1) / 2.0) / DEC
    taper = 0.5 - 0.5 * np.cos(2.0 * np.pi * (index + 0.5) / TAPS)
    taps = (np.sinc(centred) * taper / DEC).astype(np.float32)
    high, low = split_high_low(taps)
    table = np.zeros((DEC, REACHED, 2 * LANE), ml_dtypes.bfloat16)
    sample = np.arange(LANE)
    column = sample // 2 + (sample % 2) * (LANE // 2)
    for phase in range(DEC):
        for offset in range(TAPS // DEC):
            table[phase, sample + offset, column] = high[DEC * offset + phase]
            table[phase, sample + offset, LANE + column] = low[DEC * offset + phase]
    return table


def angles(left, right):
    return np.mod(left * right, LENGTH).astype(np.float64) * (2.0 * np.pi / LENGTH)


def dft_table():
    half = np.arange(LENGTH // 2)[:, None]
    bins = np.arange(HALF)[None, :]
    tables = []
    for parity in range(2):
        angle = angles(2 * half + parity, bins)
        real, imag = np.cos(angle), -np.sin(angle)
        middle = angles(2 * half + parity, BINS // 2)[:, 0]
        imag[:, 0] = -np.sin(middle) if parity else np.cos(middle)
        tables.append(np.concatenate([real, imag], axis=1).astype(np.float32))
    table = np.stack(tables).astype(ml_dtypes.bfloat16).astype(np.float32) * np.float32(SCALE)
    return table.astype(ml_dtypes.bfloat16)


def lag_table():
    bins = np.arange(BINS)
    bins = np.where(bins > HALF, BINS + HALF - bins, bins)[:, None]
    lag = np.arange(LAGS)[None, :] - LAGS // 2
    angle = angles(bins, lag)
    weights = np.where(bins == 0, 1.0, 2.0)
    table = np.concatenate([weights * np.cos(angle), -weights * np.sin(angle)], axis=0)
    return table.astype(np.float32).astype(ml_dtypes.bfloat16)


def spectra_kernel(
    raw_hbm, fir_hbm, dft_hbm, out_ref, raw_ref, fir_ref, dft_ref, wide_ref, sems
):
    def fetch(source, target, index):
        return pltpu.make_async_copy(source, target, sems.at[index])

    windows = raw_ref.shape[0] // CHUNKS
    parts = 2
    raw_copies = [
        fetch(
            raw_hbm.at[pl.ds(windows * c, windows)], raw_ref.at[pl.ds(windows * c, windows)], c
        )
        for c in range(CHUNKS)
    ]
    fir_copy = fetch(fir_hbm, fir_ref.at[:, pl.ds(0, REACHED)], CHUNKS)
    dft_copies = [
        fetch(
            dft_hbm.at[c],
            dft_ref.at[c],
            CHUNKS + 1 + c,
        )
        for c in range(parts)
    ]
    for copy in [fir_copy] + raw_copies + dft_copies:
        copy.start()
    blocks = LENGTH // LANE
    tail = raw_ref.shape[-1] - LENGTH
    wide_ref[blocks] = jnp.zeros((DEC * ROWS, LANE), f32)
    for c in range(CHUNKS):
        raw_copies[c].wait()
        for row in range(windows * SENSORS * c, windows * SENSORS * (c + 1)):
            place = slice(row * DEC, (row + 1) * DEC)
            values = raw_ref[row // SENSORS, row % SENSORS].astype(f32)
            for k in range(blocks):
                wide_ref[k, place] = values[:, LANE * k : LANE * (k + 1)]
            wide_ref[blocks, place, :tail] = values[:, LENGTH:]
    fir_ref[:, REACHED:] = jnp.zeros((DEC, 2 * LANE - REACHED, 2 * LANE), bf16)
    fir_copy.wait()
    totals = []
    for part in range(2):
        first = blocks // 2 * part
        count = blocks // 2
        columns = []
        for phase in range(DEC):
            pieces = [
                wide_ref[k, pl.ds(phase, ROWS, stride=DEC), :].astype(bf16)
                for k in range(first, first + count + 1)
            ]
            columns.append(
                jnp.concatenate(
                    [jnp.concatenate(pieces[k : k + 2], axis=1) for k in range(count)], axis=0
                )
            )
        totals.append(
            jnp.dot(
                jnp.concatenate(columns, axis=1),
                fir_ref[...].reshape(DEC * 2 * LANE, 2 * LANE),
                preferred_element_type=f32,
            )
        )
    total = jnp.concatenate(totals, axis=0)
    summed = total[:, :LANE] + total[:, LANE:]
    turned = pltpu.roll(summed, LANE // 2, 1)
    lower = lax.broadcasted_iota(jnp.int32, (ROWS, LANE), 1) < LANE // 2
    samples = ([], [])
    for k in range(0, blocks, 2):
        here = slice(ROWS * k, ROWS * (k + 1))
        there = slice(ROWS * (k + 1), ROWS * (k + 2))
        samples[0].append(jnp.where(lower, summed[here], turned[there]))
        samples[1].append(jnp.where(lower, turned[here], summed[there]))
    sums = []
    for parity in range(2):
        decimated = jnp.concatenate(samples[parity], axis=1).astype(bf16)
        dft_copies[parity].wait()
        sums.append(jnp.dot(decimated, dft_ref[parity], preferred_element_type=f32))
    even, odd = sums
    real_sum = even[:, :HALF] + odd[:, :HALF]
    real_difference = even[:, :HALF] - odd[:, :HALF]
    even_imag, odd_imag = even[:, HALF:], odd[:, HALF:]
    first = lax.broadcasted_iota(jnp.int32, (ROWS, HALF), 1) == 0
    out_ref[:, :HALF] = real_sum.astype(bf16)
    out_ref[:, HALF:BINS] = jnp.where(first, even_imag, real_difference).astype(bf16)
    out_ref[:, BINS : BINS + HALF] = jnp.where(first, 0.0, even_imag + odd_imag).astype(bf16)
    out_ref[:, BINS + HALF :] = jnp.where(first, odd_imag, odd_imag - even_imag).astype(bf16)


def in_hbm(array):
    return pltpu.with_memory_space_constraint(array, pltpu.MemorySpace.HBM)


def spectra_of(raw):
    hbm = pl.BlockSpec(memory_space=pltpu.MemorySpace.HBM)
    fir, dft = fir_table(), dft_table()
    return pl.pallas_call(
        spectra_kernel,
        out_shape=pltpu.VMEM((ROWS, LENGTH), bf16),
        in_specs=[hbm, hbm, hbm],
        out_specs=pl.BlockSpec(memory_space=VMEM),
        scratch_shapes=[
            pltpu.VMEM(raw.shape, bf16),
            pltpu.VMEM((DEC, 2 * LANE, 2 * LANE), bf16),
            pltpu.VMEM(dft.shape, bf16),
            pltpu.VMEM((LENGTH // LANE + 1, DEC * ROWS, LANE), f32),
            pltpu.SemaphoreType.DMA((2 * CHUNKS + 1,)),
        ],
        compiler_params=pltpu.CompilerParams(vmem_limit_bytes=LIMIT),
        cost_estimate=pl.CostEstimate(flops=10**5, bytes_accessed=10**4, transcendentals=0),
        name="spectra",
    )(in_hbm(raw), in_hbm(jnp.asarray(fir)), in_hbm(jnp.asarray(dft)))


def cross_body(own_ref, far_ref, store):
    for tile in range(BINS // LANE):
        real = slice(LANE * tile, LANE * (tile + 1))
        imag = slice(BINS + LANE * tile, BINS + LANE * (tile + 1))
        both = slice(LENGTH + LANE * tile, LENGTH + LANE * (tile + 1))

        def step(pair, totals):
            first, second, third, power = totals
            rows = pl.ds(pl.multiple_of(pair * 16, 16), 16)
            far_real = far_ref[rows, real].astype(f32)
            far_imag = far_ref[rows, imag].astype(f32)
            far_difference = far_real - far_imag
            first, second, third = list(first), list(second), list(third)
            for half in range(2):
                part = slice(SENSORS * half, SENSORS * (half + 1))
                power = power + (far_real[part] * far_real[part] + far_imag[part] * far_imag[part])
                for i in range(SENSORS):
                    row = pl.ds(pair * 16 + SENSORS * half + i, 1)
                    first[i] = first[i] + own_ref[row, real] * far_real[part]
                    second[i] = second[i] + own_ref[row, imag] * far_imag[part]
                    third[i] = third[i] + own_ref[row, both] * far_difference[part]
            return tuple(first), tuple(second), tuple(third), power

        zero = jnp.zeros((SENSORS, LANE), f32)
        zeros = (zero,) * SENSORS
        first, second, third, power = lax.fori_loop(
            0, WIN // 2, step, (zeros, zeros, zeros, zero), unroll=True
        )
        store(real, imag, first, second, third, power)


def put_cross(out_refs, base, real, imag, first, second, third):
    for k in range(4):
        pair = [2 * k, 2 * k + 1]
        real_cross = jnp.concatenate([first[i] + second[i] for i in pair], axis=0)
        imag_cross = jnp.concatenate([third[i] - first[i] + second[i] for i in pair], axis=0)
        out_refs[k][base : base + PAIRS, real] = real_cross.astype(bf16)
        out_refs[k][base : base + PAIRS, imag] = imag_cross.astype(bf16)


def cross_kernel(own_ref, far_ref, out_ref, power_ref):
    def store(real, imag, first, second, third, power):
        put_cross([out_ref.at[k] for k in range(4)], 0, real, imag, first, second, third)
        power_ref[:, real] = power

    cross_body(own_ref, far_ref, store)


def cross_of(own, far):
    return pl.pallas_call(
        cross_kernel,
        out_shape=(
            pltpu.VMEM((4, PAIRS, LENGTH), bf16),
            pltpu.VMEM((SENSORS, BINS), f32),
        ),
        in_specs=[pl.BlockSpec(memory_space=VMEM)] * 2,
        out_specs=(pl.BlockSpec(memory_space=VMEM),) * 2,
        compiler_params=pltpu.CompilerParams(vmem_limit_bytes=LIMIT),
        cost_estimate=pl.CostEstimate(flops=10**5, bytes_accessed=10**4, transcendentals=0),
        name="cross",
    )(own, far)


def own_kernel(turn_ref, spectra_ref, own_ref, mine_ref):
    turn = turn_ref[0]
    power = jnp.zeros((SENSORS, BINS), f32)
    sensor = lax.broadcasted_iota(jnp.int32, (SENSORS, LENGTH), 0)
    upper = lax.rem(sensor, 4) >= 2
    odd = lax.rem(turn, 2) == 1
    high = turn >= 2
    for window in range(WIN):
        rows = slice(SENSORS * window, SENSORS * (window + 1))
        block = spectra_ref[rows].astype(f32)
        swapped = jnp.where(upper, pltpu.roll(block, 2, 0), pltpu.roll(block, SENSORS - 2, 0))
        block = jnp.where(odd, swapped, block)
        block = jnp.where(high, pltpu.roll(block, 4, 0), block)
        own_ref[rows, :LENGTH] = block
        own_ref[rows, LENGTH:] = block[:, :BINS] + block[:, BINS:]
        square = block * block
        power = power + (square[:, :BINS] + square[:, BINS:])
    rounded = power.astype(bf16).astype(f32)
    mine = jnp.concatenate([rounded, power - rounded], axis=1)
    for k in range(4):
        mine_ref[k] = jnp.concatenate([mine[2 * k : 2 * k + 2]] * 4, axis=0)


def own_of(turn, spectra):
    vmem = pl.BlockSpec(memory_space=VMEM)
    return pl.pallas_call(
        own_kernel,
        out_shape=(
            pltpu.VMEM((ROWS, LENGTH + BINS), f32),
            pltpu.VMEM((4, SENSORS, LENGTH), f32),
        ),
        in_specs=[pl.BlockSpec(memory_space=pltpu.MemorySpace.SMEM), vmem],
        out_specs=(vmem, vmem),
        compiler_params=pltpu.CompilerParams(vmem_limit_bytes=LIMIT),
        cost_estimate=pl.CostEstimate(flops=10**5, bytes_accessed=10**4, transcendentals=0),
        name="own",
    )(turn, spectra)


def message_kernel(
    own_ref, far_ref, s_ref, sp_ref, a_ref, ap_ref, b_ref, bp_ref, mine_ref, *out_refs
):
    collected = []

    def store(real, imag, first, second, third, power):
        put_cross(out_refs, 3 * PAIRS, real, imag, first, second, third)
        collected.append(power)

    cross_body(own_ref, far_ref, store)
    near = jnp.concatenate(
        [
            jnp.concatenate([sp_ref[...], ap_ref[...]], axis=1),
            jnp.concatenate([bp_ref[...], jnp.concatenate(collected, axis=1)], axis=1),
        ],
        axis=0,
    ).astype(bf16)
    base = CANDS * PAIRS
    for k in range(4):
        out_refs[k][0:PAIRS] = s_ref[k]
        out_refs[k][PAIRS : 2 * PAIRS] = a_ref[k]
        out_refs[k][2 * PAIRS : 3 * PAIRS] = b_ref[k]
        out_refs[k][base : base + 16] = near
        out_refs[k][base + 16 : MESSAGE] = mine_ref[k].astype(bf16)


def messages_of(*parts):
    vmem = pl.BlockSpec(memory_space=VMEM)
    return pl.pallas_call(
        message_kernel,
        out_shape=(pltpu.VMEM((MESSAGE, LENGTH), bf16),) * 4,
        in_specs=[vmem] * len(parts),
        out_specs=(vmem,) * 4,
        compiler_params=pltpu.CompilerParams(vmem_limit_bytes=LIMIT),
        cost_estimate=pl.CostEstimate(flops=10**5, bytes_accessed=10**4, transcendentals=0),
        name="message",
    )(*parts)


def lag_kernel(tile_ref, blocks_ref, mask_ref, table_ref, *refs):
    got_refs, out_ref, lagged_ref = refs[:4], refs[4], refs[5]
    base = CANDS * PAIRS

    def summed(rows):
        parts = [ref[rows].astype(f32) for ref in got_refs]
        return (parts[0] + parts[1]) + (parts[2] + parts[3])

    def inverse(power):
        return lax.rsqrt(power / (4 * WIN) + 1e-06 * SCALE * SCALE)

    near = inverse(summed(slice(base, base + 16)))
    mine = summed(slice(base + 16, MESSAGE))
    mine = inverse(mine[:, :BINS] + mine[:, BINS:])
    own = [mine[i : i + 1] for i in range(2)]
    pieces = []
    for slot in range(CANDS):
        row, column = slot // 2, slot % 2
        far = near[SENSORS * row : SENSORS * (row + 1), BINS * column : BINS * (column + 1)]
        cross = summed(slice(slot * PAIRS, (slot + 1) * PAIRS))
        for i in range(2):
            factor = far * own[i]
            factor = jnp.concatenate([factor, factor], axis=1)
            pieces.append(cross[SENSORS * i : SENSORS * (i + 1)] * factor)
    whitened = jnp.concatenate(pieces, axis=0)
    high = whitened.astype(bf16)
    low = (whitened - high.astype(f32)).astype(bf16)
    both = jnp.concatenate([high, low], axis=0)
    lagged = jnp.dot(both, table_ref[...], preferred_element_type=f32)
    lagged = lagged[: CANDS * PAIRS] + lagged[CANDS * PAIRS :]
    lagged_ref[...] = lagged.reshape(CANDS, 2, SENSORS, LAGS)
    normaliser = 1.0 / math.sqrt(4 * WIN * BINS)
    tile = tile_ref[0]
    other = 1 - 2 * lax.rem(tile, 2)
    diagonal = lax.broadcasted_iota(jnp.int32, (SENSORS, SENSORS), 0) == (
        lax.broadcasted_iota(jnp.int32, (SENSORS, SENSORS), 1)
    )
    for r in range(4):
        relative = blocks_ref[r] - tile
        slot = jnp.where(
            relative == other,
            0,
            jnp.where(relative == -other, 3, jnp.where(relative == 2 * other, 1, 2)),
        )
        for i in range(2):
            row = mask_ref[i, r : r + 1, :].astype(f32) * normaliser
            column = jnp.sum(jnp.where(diagonal, row, 0.0), axis=1, keepdims=True)
            out_ref[i, r] = lagged_ref[slot, i] * column


def lag_of(tile, blocks, mask, *got):
    smem = pl.BlockSpec(memory_space=pltpu.MemorySpace.SMEM)
    vmem = pl.BlockSpec(memory_space=VMEM)
    table = lag_table()
    return pl.pallas_call(
        lag_kernel,
        out_shape=jax.ShapeDtypeStruct((2, 4, SENSORS, LAGS), f32),
        in_specs=[smem, smem] + [vmem] * 6,
        out_specs=vmem,
        scratch_shapes=[pltpu.VMEM((CANDS, 2, SENSORS, LAGS), f32)],
        compiler_params=pltpu.CompilerParams(vmem_limit_bytes=LIMIT),
        cost_estimate=pl.CostEstimate(flops=10**5, bytes_accessed=10**4, transcendentals=0),
        name="lag",
    )(tile, blocks, mask, jnp.asarray(table), *got)


def per_device(raw, blocks, mask):
    tiles = lax.axis_size("tile")
    tile = lax.axis_index("tile").astype(jnp.int32).reshape(1)
    turn = lax.axis_index("tm").astype(jnp.int32).reshape(1)

    def ring(block, distances):
        def target(i):
            there = i + distances[i % 2]
            return there if 0 <= there < tiles else i + 1 - 2 * (i % 2)

        return lax.ppermute(block, "tile", [(i, target(i)) for i in range(tiles)])

    def onward(block, step):
        return lax.ppermute(block, "tm", [(i, i ^ step) for i in range(lax.axis_size("tm"))])

    spectra = spectra_of(raw)
    near = ring(spectra, (1, -1))
    ahead = ring(spectra, (-2, 2))
    behind = ring(spectra, (2, -2))
    own, mine = own_of(turn, spectra)
    s_cross, s_power = cross_of(own, near)
    ahead, s_power = lax.optimization_barrier((ahead, s_power))
    corner = ring(ahead, (1, -1))
    a_cross, a_power = cross_of(own, ahead)
    b_cross, b_power = cross_of(own, behind)
    messages = messages_of(
        own, corner, s_cross, s_power, a_cross, a_power, b_cross, b_power, mine
    )
    got = [messages[0]] + [onward(messages[k], k) for k in (2, 1, 3)]
    return lag_of(tile, blocks, mask, *got)


def solution(mesh):
    placed = (P("tm", "tile", None, None), P("tile"), P("tm", "tile", None))
    return jax.shard_map(
        per_device,
        mesh=mesh,
        in_specs=placed,
        out_specs=P("tm", "tile", None, None),
        check_vma=False,
    )
```
